768 devices in a mesh: node: 12 (over z), local: 64 (over y, x, core).
Axes of the slice: x: 4, y: 8, z: 12, core: 2. Of those that a mesh axis runs over, the one named last changes fastest.
Arguments:
- inputs_x: bfloat16 [36864, 2048], P(('node', 'local')), may hold values from -6 to 6
- grad_out: bfloat16 [36864, 2048], P(('node', 'local')), may hold values from -6 to 6
- group_order: int32 [768, 12], P(('node', 'local')), may hold values from 0 to 11, each once within a row
- route_picks: int32 [36864, 1], P(('node', 'local')), may hold values from 0 to 7; in each aligned block of 48 rows (0 to 47, 48 to 95, ...) at most 6 rows name the same one
- gate_weights: bfloat16 [36864, 1], P(('node', 'local')), may hold values from 0.099609375 to 0.69921875
- w_gate: bfloat16 [393216, 512], P(('node', 'local')), may hold values from -0.125 to 0.125
- w_up: bfloat16 [393216, 512], P(('node', 'local')), may hold values from -0.125 to 0.125
- w_down: bfloat16 [393216, 512], P(('node', 'local')), may hold values from -0.1875 to 0.1875
Outputs:
- grad_x: bfloat16 [36864, 2048], P(('node', 'local'))
The draws below stay inside these ranges and needn't reach their ends.
Inputs may be any that keep to these rules, and one draw needn't show every extreme that they name: `group_order`: every row is a permutation; so each device's tokens pick each node group exactly 4 times. `route_picks`: the 1 numbers of a row differ; in each aligned block of 48 rows (the rows of one device) no number stands in more than 6 rows, and some number stands in exactly 6 rows of some block.
All inputs are finite; a program needn't handle non-finite values.
Results may differ from the reference program's by a relative error of at most 0.0065.
Values may be sent and summed in bfloat16 or wider, within the bound.
A program may use at most 32 MiB of HBM per device.

```python
import math
import jax
import jax.numpy as jnp
import numpy as np
from jax import lax

D = 2048
HID = 1024
HSPLIT = 2
GROUPS_TOK = 1
TOK_DEV = 48
PER_GROUP = 1
EXP_NODE = 8
ROWS2 = 48
CAP_G = 4
CAP2 = 6
EXPERTS = 96
TOKENS = 36864
N_NODE = 12
N_LOCAL = 64


def level_of(stream_key, extent, shards, low, high):
    factor_of = 1.0
    for dim, parts in shards:
        steps = jax.random.uniform(jax.random.fold_in(jax.random.fold_in(stream_key, 6), dim), (parts,), jnp.float32, low / len(shards), high / len(shards))
        factor_of = factor_of * jnp.repeat(jnp.exp(steps), extent[dim] // parts).reshape((-1,) + (1,) * (len(extent) - 1 - dim))
    return factor_of


def routed_block(own_key, own, number, rows, amount, top, limit, slope):
    ranking = jax.random.permutation(own_key, amount)
    crowded, usual = shares(amount, rows * top, limit, slope, True), shares(amount, rows * top, limit, slope, False)
    places = jnp.arange(amount)

    def named(lengths, offset_by):
        used = int((lengths > 0).sum())
        fixed = max(1, used // 4)
        passed = fixed + (places - fixed + offset_by * (used - fixed)) % max(1, amount - fixed)
        return jnp.zeros((amount,), jnp.int32).at[ranking[jnp.where(places < fixed, places, passed)]].set(jnp.asarray(lengths, jnp.int32))

    lengths = jnp.where(number % 4 == 0, named(crowded, number // 4), named(usual, number - number // 4 - 1))
    mixed = jax.random.permutation(jax.random.fold_in(own, 3), amount)
    source_of, sink = mixed[0:amount // 2 * 2:2], mixed[1:amount // 2 * 2:2]
    margin = jnp.minimum(lengths[source_of] - 1, limit - lengths[sink]) // 2
    margin = jnp.where((source_of == ranking[0]) | (sink == ranking[0]) | (lengths[sink] == 0), 0, jnp.maximum(margin, 0))
    passed = jax.random.randint(jax.random.fold_in(own, 4), (amount // 2,), 0, 1 << 20) % (margin + 1)
    lengths = lengths.at[source_of].add(-passed).at[sink].add(passed)
    members = jnp.searchsorted(jnp.cumsum(lengths), jnp.arange(rows * top), side="right").astype(jnp.int32)
    listing = members.reshape(top, rows).T
    listing = listing[jax.random.permutation(jax.random.fold_in(own, 1), rows)]
    offset_by = jax.random.randint(jax.random.fold_in(own, 2), (rows, 1), 0, top)
    return jnp.take_along_axis(listing, (jnp.arange(top)[None, :] + offset_by) % top, axis=1)


def shares(amount, total, most, slope, full):
    weights = [(1 << 20) // math.isqrt(rank ** slope) + 1 for rank in range(1, amount + 1)]
    largest = most if full else min(most, max(-(-total // amount), total * weights[0] // sum(weights)))
    least = 1 if total - largest >= amount - 1 else 0
    counts, rest = [largest] + [least] * (amount - 1), total - largest - least * (amount - 1)
    while rest > 0:
        candidates = [i for i in range(1, amount) if counts[i] < largest] or [i for i in range(1, amount) if counts[i] < most]
        mass, left = sum([weights[i] for i in candidates]), rest
        for i in candidates:
            addition = min(most - counts[i], max(1, left * weights[i] // mass), rest)
            counts[i] = counts[i] + addition
            rest = rest - addition
    return np.array(counts)


def centred(own_key, extent, scale, most, cuts=(), held_as=jnp.bfloat16):
    drawn = jax.random.normal(own_key, extent, jnp.float32) * scale
    if len(cuts) > 0:
        drawn = level_of(own_key, extent, cuts, -0.22, 0.18) * drawn
    return jnp.clip(drawn, min=-most, max=most).astype(held_as)


def setup_inputs(seed: int = 0) -> dict:
    arg_keys = jax.random.split(jax.random.key(seed), 9)
    inputs_x = centred(arg_keys[0], (TOKENS, D), 1.0, 6.0, ((0, 768),))
    grad_out = centred(arg_keys[1], (TOKENS, D), 1.0, 6.0, ((0, 768),))
    group_order = jax.vmap(lambda own: jax.random.permutation(own, N_NODE))(jax.random.split(arg_keys[2], (N_NODE * N_LOCAL))).reshape((N_NODE * N_LOCAL, N_NODE)).astype(jnp.int32)
    route_picks_keys = jax.random.split(jax.random.fold_in(arg_keys[3], 1), (N_NODE * N_LOCAL * ROWS2) // ROWS2)
    route_picks_turns = jax.random.permutation(jax.random.fold_in(arg_keys[3], 3), (N_NODE * N_LOCAL * ROWS2) // ROWS2)
    route_picks = jax.vmap(lambda own, number: routed_block(jax.random.fold_in(arg_keys[3], 2), own, number, ROWS2, EXP_NODE, PER_GROUP, CAP2, 2))(route_picks_keys, route_picks_turns).reshape((N_NODE * N_LOCAL * ROWS2, PER_GROUP))
    gate_weights = jnp.clip(0.099609375 + 0.5996094 * jax.random.uniform(arg_keys[4], (N_NODE * N_LOCAL * ROWS2, PER_GROUP), jnp.float32) ** level_of(arg_keys[4], (N_NODE * N_LOCAL * ROWS2, PER_GROUP), ((0, 768),), -0.2, 0.2), 0.099609375, 0.69921875).astype(jnp.bfloat16)
    w_gate = centred(arg_keys[5], (EXPERTS * HSPLIT * D, HID // HSPLIT), D ** -0.5, 0.125, ((0, 768),))
    w_up = centred(arg_keys[6], (EXPERTS * HSPLIT * D, HID // HSPLIT), D ** -0.5, 0.125, ((0, 768),))
    w_down = centred(arg_keys[7], (EXPERTS * HSPLIT * D, HID // HSPLIT), HID ** -0.5, 0.1875, ((0, 768),))
    return {"inputs_x": inputs_x, "grad_out": grad_out, "group_order": group_order, "route_picks": route_picks, "gate_weights": gate_weights, "w_gate": w_gate, "w_up": w_up, "w_down": w_down}


def reference(inputs_x, grad_out, group_order, route_picks, gate_weights, w_gate, w_up, w_down):
    half_width = HID // HSPLIT
    row_total = N_NODE * N_LOCAL * ROWS2
    slot_count = N_LOCAL * CAP2
    group_ids = jnp.arange(N_NODE, dtype=jnp.int32)
    position = jnp.sum(jnp.where(group_order[:, None, :] == group_ids[None, :, None], group_ids[None, None, :], 0), axis=2).astype(jnp.int32)
    row_ids = jnp.arange(ROWS2, dtype=jnp.int32)
    local_ids = jnp.arange(N_LOCAL, dtype=jnp.int32)
    source_dev = (row_ids[None, None, :] // CAP_G) * N_LOCAL + local_ids[None, :, None] + 0 * group_ids[:, None, None]
    group_full = group_ids[:, None, None] + 0 * source_dev
    placed = (row_ids[None, None, :] % CAP_G) * N_NODE + position[source_dev, group_full]
    token_of_row = (source_dev * TOK_DEV + placed // GROUPS_TOK).reshape(row_total).astype(jnp.int32)
    flat_pick = route_picks.reshape(N_NODE, N_LOCAL, ROWS2 * PER_GROUP)
    onehot = (flat_pick[..., None] == jnp.arange(EXP_NODE, dtype=jnp.int32)).astype(jnp.int32)
    before = jnp.cumsum(onehot, axis=2) - onehot
    slot_rank = jnp.sum(before * onehot, axis=3)
    expert = (group_ids[:, None, None] * EXP_NODE + flat_pick).reshape(row_total * PER_GROUP).astype(jnp.int32)
    slot_pos = (local_ids[None, :, None] * CAP2 + slot_rank).reshape(row_total * PER_GROUP).astype(jnp.int32)
    pair_row = jnp.repeat(jnp.arange(row_total, dtype=jnp.int32), PER_GROUP)
    pair_token = token_of_row[pair_row]
    token_table = jnp.full((EXPERTS, slot_count), TOKENS, jnp.int32).at[expert, slot_pos].set(pair_token)
    row_table = jnp.full((EXPERTS, slot_count), row_total, jnp.int32).at[expert, slot_pos].set(pair_row)
    gate_table = jnp.zeros((EXPERTS, slot_count), jnp.float32).at[expert, slot_pos].set(gate_weights.reshape(row_total * PER_GROUP).astype(jnp.float32))
    gate_mats = w_gate.reshape(EXPERTS, HSPLIT, D, half_width)
    up_mats = w_up.reshape(EXPERTS, HSPLIT, D, half_width)
    down_mats = w_down.reshape(EXPERTS, HSPLIT, D, half_width)
    pad_x = jnp.concatenate([inputs_x, jnp.zeros((1, D), jnp.bfloat16)], axis=0)
    pad_y = jnp.concatenate([grad_out, jnp.zeros((1, D), jnp.bfloat16)], axis=0)
    column_dims = (((1,), (1,)), ((), ()))

    def expert_step(totals, item):
        token_list, row_list, gate_list, gate_mat, up_mat, down_mat = item
        rows_x = pad_x[token_list]
        rows_y = pad_y[token_list]
        dout = (gate_list[:, None] * rows_y.astype(jnp.float32)).astype(jnp.bfloat16)
        summed = jnp.zeros((slot_count, D), jnp.float32)
        for part_num in range(HSPLIT):
            pre_gate = jnp.dot(rows_x, gate_mat[part_num], preferred_element_type=jnp.float32)
            pre_up = jnp.dot(rows_x, up_mat[part_num], preferred_element_type=jnp.float32)
            grad_hid = jnp.dot(dout, down_mat[part_num], preferred_element_type=jnp.float32)
            sigmoid_gate = jax.nn.sigmoid(pre_gate)
            d_gate = (grad_hid * pre_up * sigmoid_gate * (1.0 + pre_gate * (1.0 - sigmoid_gate))).astype(jnp.bfloat16)
            d_up = (grad_hid * pre_gate * sigmoid_gate).astype(jnp.bfloat16)
            contrib = lax.dot_general(d_gate, gate_mat[part_num], column_dims, preferred_element_type=jnp.float32)
            contrib = contrib + lax.dot_general(d_up, up_mat[part_num], column_dims, preferred_element_type=jnp.float32)
            summed = summed + contrib.astype(jnp.bfloat16).astype(jnp.float32)
        totals = totals.at[row_list].add(summed)
        return totals, None

    start_totals = jnp.zeros((row_total + 1, D), jnp.float32)
    totals, unused = lax.scan(expert_step, start_totals, (token_table, row_table, gate_table, gate_mats, up_mats, down_mats))
    group_part = totals[:row_total].astype(jnp.bfloat16)
    grad_x = jnp.zeros((TOKENS, D), jnp.float32).at[token_of_row].add(group_part.astype(jnp.float32)).astype(jnp.bfloat16)
    return grad_x
```

```python
import jax
import jax.numpy as jnp
from jax import lax
from jax.experimental import pallas as pl
from jax.experimental.pallas import tpu as pltpu
from jax.sharding import PartitionSpec as P

MESH = pl.DeviceIdType.MESH
BF16 = jnp.bfloat16
F32 = jnp.float32
I32 = jnp.int32

NZ, NY, NX = 12, 8, 4
TOK = 48
CAP_G, CAP_E = 4, 6
LT = 8
LANES = 128
ROWS = TOK * LT
HALF = 512
PLANE = NY * NX


def one_hot(key):
    rows = lax.broadcasted_iota(I32, (ROWS, ROWS), 0)
    return jnp.where(rows == key, 1.0, 0.0).astype(BF16)


def reorder(matrix, value):
    return jnp.dot(matrix, value, preferred_element_type=F32).astype(BF16)


def drain(ref, sem):
    pltpu.make_async_copy(ref, ref, sem).wait()


def kernel(
    order_ref, picks_ref, gates_ref, x_hbm, y_hbm, wg_hbm, wu_hbm, wd_hbm, out_ref,
    rows_in, zsend, zrecv, ysend, yrecv, lhs, wbuf, part, part_out, part_in, rsend, rrecv, stage,
    bsend, brecv, p_grp, p_exp, p_expw, p_mat, p_mat_t, p_exp_t, p_grp_t,
    in_sem, w_sem, ws_sem, wr_sem, zs_sem, zr_sem, ys_sem, yr_sem, ps_sem, pr_sem, rs_sem, rr_sem, bs_sem, br_sem,
):
    node = lax.axis_index("node")
    local = lax.axis_index("local")
    core = lax.rem(local, 2)
    my_x = lax.rem(lax.div(local, 2), NX)
    my_y = lax.div(local, 2 * NX)
    here = my_y * NX + my_x
    my_h, my_k = lax.div(my_x, 2), lax.rem(my_x, 2)

    def place(y, x):
        return (node, (y * NX + x) * 2 + core)

    def plane_peer(step):
        spot = lax.rem(here + step, PLANE)
        return lax.div(spot, NX), lax.rem(spot, NX)

    barrier = pltpu.get_barrier_semaphore()

    @pl.loop(1, NZ)
    def _(step):
        pl.semaphore_signal(
            barrier, inc=1, device_id=(lax.rem(node + step, NZ), local), device_id_type=MESH
        )

    @pl.loop(1, PLANE)
    def _(step):
        y, x = plane_peer(step)
        pl.semaphore_signal(barrier, inc=1, device_id=place(y, x), device_id_type=MESH)

    twin = (node, local + 1 - 2 * core)
    pl.semaphore_signal(barrier, inc=1, device_id=twin, device_id_type=MESH)

    load_x = pltpu.make_async_copy(x_hbm, rows_in.at[0], in_sem.at[0])
    load_y = pltpu.make_async_copy(y_hbm, rows_in.at[1], in_sem.at[1])
    load_x.start()
    load_y.start()
    loads_w = [
        pltpu.make_async_copy(w, wbuf.at[m, core], w_sem.at[m])
        for m, w in enumerate((wg_hbm, wu_hbm, wd_hbm))
    ]
    for load in loads_w:
        load.start()

    lane = lax.broadcasted_iota(I32, (1, ROWS), 1)
    tok_b, tok_t = lax.div(lane, TOK), lax.rem(lane, TOK)
    turn = lax.rem(tok_t, NZ)
    group = jnp.zeros((1, ROWS), I32)
    for k in range(NZ):
        group = jnp.where(turn == k, order_ref[0, k], group)
    p_grp[...] = one_hot(group * (LT * CAP_G) + tok_b * CAP_G + lax.div(tok_t, NZ))

    def pack(arr):
        for b in range(LT):
            for f in range(2):
                stage[arr, b * TOK : (b + 1) * TOK, f * LANES : (f + 1) * LANES] = rows_in[
                    arr, :, (f * LT + b) * LANES : (f * LT + b + 1) * LANES
                ]
        zsend[arr] = reorder(p_grp[...], stage[arr]).reshape(NZ, LT * CAP_G, 2 * LANES)

    def start_z(src, dst, s_sem, r_sem):
        @pl.loop(1, NZ)
        def _(step):
            g = lax.rem(node + step, NZ)
            pltpu.make_async_remote_copy(
                src_ref=src.at[g], dst_ref=dst.at[node], send_sem=s_sem, recv_sem=r_sem,
                device_id=(g, local), device_id_type=MESH,
            ).start()

        pltpu.make_async_copy(src.at[node], dst.at[node], r_sem).start()

    load_x.wait()
    pack(0)
    pl.semaphore_wait(barrier, NZ - 1 + PLANE - 1 + 1)
    start_z(zsend.at[0], zrecv.at[0], zs_sem.at[0], zr_sem.at[0])
    load_y.wait()
    pack(1)
    start_z(zsend.at[1], zrecv.at[1], zs_sem.at[1], zr_sem.at[1])

    sends_w = [
        pltpu.make_async_remote_copy(
            src_ref=w, dst_ref=wbuf.at[m, core], send_sem=ws_sem.at[m], recv_sem=wr_sem.at[m],
            device_id=twin, device_id_type=MESH,
        )
        for m, w in enumerate((wg_hbm, wu_hbm, wd_hbm))
    ]
    for send in sends_w:
        send.start()

    picks = picks_ref[...].astype(F32)
    row48 = lax.broadcasted_iota(I32, (TOK, TOK), 0)
    col48 = lax.broadcasted_iota(I32, (TOK, TOK), 1)
    picks_lane = jnp.sum(jnp.where(row48 == col48, picks, 0.0), axis=0, keepdims=True)
    same = (picks == picks_lane) & (col48 < row48)
    rank = jnp.sum(jnp.where(same, 1.0, 0.0), axis=1, keepdims=True)
    grp_n, grp_b, grp_c = lax.div(lane, LT * CAP_G), lax.rem(lax.div(lane, CAP_G), LT), lax.rem(lane, CAP_G)
    row_id = lax.broadcasted_iota(I32, (TOK, ROWS), 0)
    mine = row_id == grp_n * CAP_G + grp_c
    slot_key = jnp.sum(jnp.where(mine, picks * (LT * CAP_E) + rank, 0.0), axis=0, keepdims=True).astype(I32)
    slot_key = slot_key + grp_b * CAP_E
    gate = jnp.sum(jnp.where(mine, gates_ref[...].astype(F32), 0.0), axis=0, keepdims=True)
    p_exp[...] = one_hot(slot_key)
    rows2d = lax.broadcasted_iota(I32, (ROWS, ROWS), 0)
    p_expw[...] = jnp.where(rows2d == slot_key, gate, 0.0).astype(BF16)
    exp_e, exp_b, exp_r = (
        lax.div(lane, LT * CAP_E), lax.rem(lax.div(lane, CAP_E), LT), lax.rem(lane, CAP_E),
    )
    p_mat[...] = one_hot(exp_b * TOK + exp_e * CAP_E + exp_r)
    mat_b, mat_y, mat_r = (
        lax.div(lane, TOK), lax.div(lax.rem(lane, TOK), CAP_E), lax.rem(lane, CAP_E),
    )
    p_mat_t[...] = one_hot(mat_y * (LT * CAP_E) + mat_b * CAP_E + mat_r)

    def start_plane(pick_src, pick_dst, own_src, own_dst, s_sem, r_sem):
        @pl.loop(1, PLANE)
        def _(step):
            y, x = plane_peer(step)
            pltpu.make_async_remote_copy(
                src_ref=pick_src(y, x), dst_ref=pick_dst, send_sem=s_sem, recv_sem=r_sem,
                device_id=place(y, x), device_id_type=MESH,
            ).start()

        pltpu.make_async_copy(own_src, own_dst, r_sem).start()

    def dispatch(arr, matrix):
        drain(zrecv.at[arr], zr_sem.at[arr])
        sorted_rows = reorder(matrix[...], zrecv[arr].reshape(ROWS, 2 * LANES))
        for f in range(2):
            ysend[arr, f] = sorted_rows[:, f * LANES : (f + 1) * LANES].reshape(NY, LT * CAP_E, LANES)
        start_plane(
            lambda y, x: ysend.at[arr, lax.rem(x, 2), y], yrecv.at[arr, my_x, my_y],
            ysend.at[arr, my_k, my_y], yrecv.at[arr, my_x, my_y], ys_sem.at[arr], yr_sem.at[arr],
        )

    dispatch(0, p_exp)
    dispatch(1, p_expw)

    wanted = lax.broadcasted_iota(I32, (TOK, ROWS), 0).astype(F32)
    slot_of_row = (picks * CAP_E + rank).astype(I32)
    here48 = slot_of_row == exp_e * CAP_E + exp_r
    source = jnp.sum(jnp.where(here48, wanted, 0.0), axis=0, keepdims=True).astype(I32)
    p_exp_t[...] = one_hot(
        lax.div(source, CAP_G) * (LT * CAP_G) + exp_b * CAP_G + lax.rem(source, CAP_G)
    )
    position = jnp.zeros((1, ROWS), I32)
    for k in range(NZ):
        position = jnp.where(grp_n == order_ref[0, k], k, position)
    p_grp_t[...] = one_hot(grp_b * TOK + grp_c * NZ + position)

    def gather_rows(arr):
        drain(yrecv.at[arr], yr_sem.at[arr])
        for pair in range(NX // 2):
            value = jnp.concatenate(
                [yrecv[arr, 2 * pair + i].reshape(ROWS, LANES) for i in range(2)], axis=1
            )
            ordered = reorder(p_mat[...], value)
            for i in range(2):
                for b in range(LT):
                    lhs[arr, (2 * pair + i) * TOK : (2 * pair + i + 1) * TOK, b * LANES : (b + 1) * LANES] = (
                        ordered[b * TOK : (b + 1) * TOK, i * LANES : (i + 1) * LANES]
                    )

    partner = place(my_y, my_x + 1 - 2 * my_k)

    def part_copy(m):
        return pltpu.make_async_remote_copy(
            src_ref=part_out.at[m], dst_ref=part_in.at[m], send_sem=ps_sem.at[m], recv_sem=pr_sem.at[m],
            device_id=partner, device_id_type=MESH,
        )

    def project(arr, m):
        value = jnp.dot(lhs[arr], wbuf[m].reshape(2 * HALF, HALF), preferred_element_type=F32)
        part[m] = value
        part_out[m] = value.astype(BF16)
        part_copy(m).start()

    def weights_ready(m):
        loads_w[m].wait()
        sends_w[m].wait_recv()

    gather_rows(0)
    for m in range(2):
        weights_ready(m)
        project(0, m)
    gather_rows(1)
    weights_ready(2)
    project(1, 2)

    for m in range(3):
        part_copy(m).wait_recv()
    pre_gate = part[0] + part_in[0].astype(F32)
    pre_up = part[1] + part_in[1].astype(F32)
    grad_hid = part[2] + part_in[2].astype(F32)
    sig = jax.nn.sigmoid(pre_gate)
    d_gate = (grad_hid * pre_up * sig * (1.0 + pre_gate * (1.0 - sig))).astype(BF16)
    d_up = (grad_hid * pre_gate * sig).astype(BF16)
    dims = (((1,), (1,)), ((), ()))
    contrib = lax.dot_general(d_gate, wbuf[0].reshape(2 * HALF, HALF), dims, preferred_element_type=F32)
    contrib = contrib + lax.dot_general(
        d_up, wbuf[1].reshape(2 * HALF, HALF), dims, preferred_element_type=F32
    )
    contrib = contrib.astype(BF16)
    for pair in range(NX // 2):
        for i in range(2):
            for b in range(LT):
                stage[pair, b * TOK : (b + 1) * TOK, i * LANES : (i + 1) * LANES] = contrib[
                    (2 * pair + i) * TOK : (2 * pair + i + 1) * TOK, b * LANES : (b + 1) * LANES
                ]
        ordered = reorder(p_mat_t[...], stage[pair])
        for i in range(2):
            rsend[(2 * pair + i) * NY : (2 * pair + i + 1) * NY] = ordered[
                :, i * LANES : (i + 1) * LANES
            ].reshape(NY, LT * CAP_E, LANES)
    start_plane(
        lambda y, x: rsend.at[x * NY + y], rrecv.at[my_h, my_k, my_y],
        rsend.at[my_x * NY + my_y], rrecv.at[my_h, my_k, my_y], rs_sem, rr_sem,
    )
    drain(rrecv, rr_sem)
    home = jnp.concatenate(
        [
            (rrecv[0, f].astype(F32) + rrecv[1, f].astype(F32)).astype(BF16).reshape(ROWS, LANES)
            for f in range(2)
        ],
        axis=1,
    )
    bsend[...] = reorder(p_exp_t[...], home).reshape(NZ, LT * CAP_G, 2 * LANES)
    start_z(bsend, brecv, bs_sem, br_sem)
    drain(brecv, br_sem)
    result = reorder(p_grp_t[...], brecv[...].reshape(ROWS, 2 * LANES))
    for f in range(2):
        for b in range(LT):
            out_ref[:, (f * LT + b) * LANES : (f * LT + b + 1) * LANES] = result[
                b * TOK : (b + 1) * TOK, f * LANES : (f + 1) * LANES
            ]

    sent_z = zsend.at[0, pl.ds(0, NZ - 1)]
    drain(sent_z, zs_sem.at[0])
    drain(sent_z, zs_sem.at[1])
    drain(bsend.at[pl.ds(0, NZ - 1)], bs_sem)
    for send in sends_w:
        send.wait_send()
    for m in range(3):
        part_copy(m).wait_send()
    for sem in (ys_sem.at[0], ys_sem.at[1], rs_sem):
        drain(rsend.at[pl.ds(0, PLANE - 1)], sem)


def per_device(inputs_x, grad_out, group_order, route_picks, gate_weights, w_gate, w_up, w_down):
    vmem = pl.BlockSpec(memory_space=pltpu.VMEM)
    hbm = pl.BlockSpec(memory_space=pl.ANY)
    square = pltpu.VMEM((ROWS, ROWS), BF16)
    dma = pltpu.SemaphoreType.DMA
    return pl.pallas_call(
        kernel,
        out_shape=jax.ShapeDtypeStruct(inputs_x.shape, BF16),
        in_specs=[pl.BlockSpec(memory_space=pltpu.SMEM), vmem, vmem] + [hbm] * 5,
        out_specs=vmem,
        scratch_shapes=[
            pltpu.VMEM((2, TOK, 2 * LT * LANES), BF16),
            pltpu.VMEM((2, NZ, LT * CAP_G, 2 * LANES), BF16),
            pltpu.VMEM((2, NZ, LT * CAP_G, 2 * LANES), BF16),
            pltpu.VMEM((2, 2, NY, LT * CAP_E, LANES), BF16),
            pltpu.VMEM((2, NX, NY, LT * CAP_E, LANES), BF16),
            pltpu.VMEM((2, NX * TOK, LT * LANES), BF16),
            pltpu.VMEM((3, 2, HALF, HALF), BF16),
            pltpu.VMEM((3, NX * TOK, HALF), F32),
            pltpu.VMEM((3, NX * TOK, HALF), BF16),
            pltpu.VMEM((3, NX * TOK, HALF), BF16),
            pltpu.VMEM((PLANE, LT * CAP_E, LANES), BF16),
            pltpu.VMEM((2, 2, NY, LT * CAP_E, LANES), BF16),
            pltpu.VMEM((2, ROWS, 2 * LANES), BF16),
            pltpu.VMEM((NZ, LT * CAP_G, 2 * LANES), BF16),
            pltpu.VMEM((NZ, LT * CAP_G, 2 * LANES), BF16),
            square, square, square, square, square, square, square,
            dma((2,)), dma((3,)), dma((3,)), dma((3,)),
            dma((2,)), dma((2,)), dma((2,)), dma((2,)),
            dma((3,)), dma((3,)), dma(()), dma(()), dma(()), dma(()),
        ],
        compiler_params=pltpu.CompilerParams(
            collective_id=0, has_side_effects=True, vmem_limit_bytes=40 * 2**20
        ),
    )(group_order, route_picks, gate_weights, inputs_x, grad_out, w_gate, w_up, w_down)


def solution(mesh):
    placed = P(("node", "local"), None)
    return jax.shard_map(
        per_device, mesh=mesh, in_specs=(placed,) * 8, out_specs=placed, check_vma=False
    )
```

```python
import jax
import jax.numpy as jnp
from jax import lax
from jax.experimental import pallas as pl
from jax.experimental.pallas import tpu as pltpu
from jax.sharding import PartitionSpec as P

MESH = pl.DeviceIdType.MESH
BF16 = jnp.bfloat16
F32 = jnp.float32
I32 = jnp.int32

NZ, NY, NX = 12, 8, 4
TOK = 48
CAP_G, CAP_E = 4, 6
LANES = 128
BLK = 8
FB = 4
ROWS = TOK * BLK
HALF = 512
QUART = 256


def one_hot(key):
    rows = lax.broadcasted_iota(I32, (ROWS, ROWS), 0)
    return jnp.where(rows == key, 1.0, 0.0).astype(BF16)


def reorder(matrix, value):
    return jnp.dot(matrix, value, preferred_element_type=F32).astype(BF16)


def column(row, size):
    shape = (size, row.shape[1])
    diag = lax.broadcasted_iota(I32, shape, 0) == lax.broadcasted_iota(I32, shape, 1)
    return jnp.sum(jnp.where(diag, row, 0.0), axis=1, keepdims=True)


def spread(values, index):
    shape = (values.shape[0], index.shape[1])
    hit = lax.broadcasted_iota(I32, shape, 0) == index
    return jnp.sum(jnp.where(hit, values, 0.0), axis=0, keepdims=True)


def drain(ref, sem):
    pltpu.make_async_copy(ref, ref, sem).wait()


def kernel(
    order_hbm, picks_hbm, gates_hbm, x_hbm, y_hbm, wg_hbm, wu_hbm, wd_hbm, out_ref,
    order_ref, picks_ref, gates_ref, rows_in, stage, zsend, zrecv, ysend, yrecv, xsend, xrecv, lhs,
    wbuf, part, part_out, part_in, rsend, rrecv, qsend, qrecv, bsend, brecv,
    p_grp, p_exp, p_expw, p_mat, p_mat_t, p_exp_t, p_grp_t,
    in_sem, wa_sem, wb_sem, wo_sem, ws_sem, wr_sem, zs_sem, zr_sem, ys_sem, yr_sem, xs_sem, xr_sem,
    ps_sem, pr_sem, rs_sem, rr_sem, qs_sem, qr_sem, bs_sem, br_sem,
):
    node = lax.axis_index("node")
    local = lax.axis_index("local")
    core = lax.rem(local, 2)
    my_x = lax.rem(lax.div(local, 2), NX)
    my_y = lax.div(local, 2 * NX)
    my_h, my_k = lax.div(my_x, 2), lax.rem(my_x, 2)

    def place(y, x):
        return (node, (y * NX + x) * 2 + core)

    z_peers = [lax.rem(node + step, NZ) for step in (6, 5, 7, 4, 8, 3, 9, 2, 10, 1, 11)]
    y_peers = [lax.rem(my_y + step, NY) for step in (4, 3, 5, 2, 6, 1, 7)]
    x_peers = [lax.rem(my_x + step, NX) for step in (2, 1, 3)]
    twin = (node, local + 1 - 2 * core)

    load_x = pltpu.make_async_copy(x_hbm, rows_in.at[0], in_sem.at[0])
    load_y = pltpu.make_async_copy(y_hbm, rows_in.at[1], in_sem.at[1])
    small = [
        pltpu.make_async_copy(src, dst, in_sem.at[2 + i])
        for i, (src, dst) in enumerate(
            ((order_hbm, order_ref), (picks_hbm, picks_ref), (gates_hbm, gates_ref))
        )
    ]
    small[0].start()
    load_x.start()
    load_y.start()
    small[1].start()
    small[2].start()

    barrier = pltpu.get_barrier_semaphore()

    def greet(device):
        pl.semaphore_signal(barrier, inc=1, device_id=device, device_id_type=MESH)

    for z in z_peers:
        greet((z, local))
    for y in y_peers:
        greet(place(y, my_x))
    for x in x_peers:
        greet(place(my_y, x))
    greet(twin)

    lane = lax.broadcasted_iota(I32, (1, ROWS), 1)
    tok_k, tok_t = lax.div(lane, TOK), lax.rem(lane, TOK)
    small[0].wait()
    order = column(order_ref[...].astype(F32), 16)
    group = spread(order, lax.rem(tok_t, NZ)).astype(I32)
    p_grp[...] = one_hot(group * (BLK * CAP_G) + tok_k * CAP_G + lax.div(tok_t, NZ))

    def feature(f, s, b):
        start = f * 2 * HALF + s * HALF + b * LANES
        return slice(start, start + LANES)

    def blocks():
        return [(f, b) for f in range(2) for b in range(FB)]

    def pack(arr):
        for k, (f, b) in enumerate(blocks()):
            for s in range(2):
                stage[arr, k * TOK : (k + 1) * TOK, s * LANES : (s + 1) * LANES] = rows_in[
                    arr, :, feature(f, s, b)
                ]
        packed = reorder(p_grp[...], stage[arr])
        for s in range(2):
            zsend[2 * arr + s] = packed[:, s * LANES : (s + 1) * LANES].reshape(NZ, BLK * CAP_G, LANES)

    def send(src, dst, s_sem, r_sem, device):
        pltpu.make_async_remote_copy(
            src_ref=src, dst_ref=dst, send_sem=s_sem, recv_sem=r_sem, device_id=device, device_id_type=MESH
        ).start()

    def start_z(src, dst, s_sem, r_sem):
        for z in z_peers:
            send(src.at[z], dst.at[node], s_sem, r_sem, (z, local))
        pltpu.make_async_copy(src.at[node], dst.at[node], r_sem).start()

    def start_y(src, dst, s_sem, r_sem):
        for y in y_peers:
            send(src.at[y], dst.at[my_y], s_sem, r_sem, place(y, my_x))
        pltpu.make_async_copy(src.at[my_y], dst.at[my_y], r_sem).start()

    def start_x(src_of, dst, s_sem, r_sem):
        for x in x_peers:
            send(src_of(x), dst.at[my_x], s_sem, r_sem, place(my_y, x))
        pltpu.make_async_copy(src_of(my_x), dst.at[my_x], r_sem).start()

    load_x.wait()
    pack(0)
    pl.semaphore_wait(barrier, NZ - 1 + NY - 1 + NX - 1 + 1)
    for k in range(2):
        start_z(zsend.at[k], zrecv.at[k], zs_sem.at[k], zr_sem.at[k])
    load_y.wait()
    pack(1)
    for k in range(2, 4):
        start_z(zsend.at[k], zrecv.at[k], zs_sem.at[k], zr_sem.at[k])

    keep = pl.multiple_of(my_h * QUART, QUART)
    other = pl.multiple_of(QUART - my_h * QUART, QUART)
    weights = (wg_hbm, wu_hbm, wd_hbm)
    kept = [
        pltpu.make_async_copy(
            w.at[:, pl.ds(keep, QUART)], wbuf.at[m, core, :, pl.ds(keep, QUART)], wa_sem.at[m]
        )
        for m, w in enumerate(weights)
    ]
    swapped = [
        pltpu.make_async_remote_copy(
            src_ref=w.at[:, pl.ds(other, QUART)], dst_ref=wbuf.at[m, core, :, pl.ds(keep, QUART)],
            send_sem=wo_sem.at[m], recv_sem=wb_sem.at[m],
            device_id=place(my_y, lax.rem(my_x + 2, NX)), device_id_type=MESH,
        )
        for m, w in enumerate(weights)
    ]
    for m, w in enumerate(weights):
        kept[m].start()

        @pl.when(my_k == 0)
        def _():
            pltpu.make_async_copy(
                w.at[:, pl.ds(other, QUART)], wbuf.at[m, core, :, pl.ds(other, QUART)], wb_sem.at[m]
            ).start()

        @pl.when(my_k == 1)
        def _():
            swapped[m].start()

    twins = [
        pltpu.make_async_remote_copy(
            src_ref=wbuf.at[m, core], dst_ref=wbuf.at[m, core], send_sem=ws_sem.at[m], recv_sem=wr_sem.at[m],
            device_id=twin, device_id_type=MESH,
        )
        for m in range(3)
    ]

    small[1].wait()
    small[2].wait()
    picks_lane = picks_ref[...].astype(F32)
    picks = column(picks_lane, TOK)
    row48 = lax.broadcasted_iota(I32, (TOK, TOK), 0)
    col48 = lax.broadcasted_iota(I32, (TOK, TOK), 1)
    same = (picks == picks_lane) & (col48 < row48)
    rank = jnp.sum(jnp.where(same, 1.0, 0.0), axis=1, keepdims=True)
    grp_n, grp_k, grp_c = lax.div(lane, BLK * CAP_G), lax.rem(lax.div(lane, CAP_G), BLK), lax.rem(lane, CAP_G)
    grp_row = grp_n * CAP_G + grp_c
    slot_key = spread(picks * (BLK * CAP_E) + rank, grp_row).astype(I32) + grp_k * CAP_E
    gate = spread(column(gates_ref[...].astype(F32), TOK), grp_row)
    p_exp[...] = one_hot(slot_key)
    rows2d = lax.broadcasted_iota(I32, (ROWS, ROWS), 0)
    p_expw[...] = jnp.where(rows2d == slot_key, gate, 0.0).astype(BF16)
    exp_e, exp_k, exp_r = (
        lax.div(lane, BLK * CAP_E), lax.rem(lax.div(lane, CAP_E), BLK), lax.rem(lane, CAP_E),
    )
    p_mat[...] = one_hot(exp_k * TOK + exp_e * CAP_E + exp_r)
    mat_k, mat_y, mat_r = (
        lax.div(lane, TOK), lax.div(lax.rem(lane, TOK), CAP_E), lax.rem(lane, CAP_E),
    )
    p_mat_t[...] = one_hot(mat_y * (BLK * CAP_E) + mat_k * CAP_E + mat_r)
    row_id = lax.broadcasted_iota(I32, (TOK, ROWS), 0).astype(F32)
    wanted = (exp_e * CAP_E + exp_r).astype(F32)
    source = jnp.sum(
        jnp.where(picks * CAP_E + rank == wanted, row_id, 0.0), axis=0, keepdims=True
    ).astype(I32)
    p_exp_t[...] = one_hot(
        lax.div(source, CAP_G) * (BLK * CAP_G) + exp_k * CAP_G + lax.rem(source, CAP_G)
    )
    turn_id = lax.broadcasted_iota(I32, (16, ROWS), 0)
    at_group = (order == grp_n.astype(F32)) & (turn_id < NZ)
    position = jnp.sum(
        jnp.where(at_group, turn_id.astype(F32), 0.0), axis=0, keepdims=True
    ).astype(I32)
    p_grp_t[...] = one_hot(grp_k * TOK + grp_c * NZ + position)

    def dispatch(k, matrix):
        drain(zrecv.at[k], zr_sem.at[k])
        ysend[k] = reorder(matrix[...], zrecv[k].reshape(ROWS, LANES)).reshape(NY, BLK * CAP_E, LANES)
        start_y(ysend.at[k], yrecv.at[k], ys_sem.at[k], yr_sem.at[k])

    def forward(k):
        drain(yrecv.at[k], yr_sem.at[k])
        xsend[k] = reorder(p_mat[...], yrecv[k].reshape(ROWS, LANES)).reshape(2, FB * TOK, LANES)
        start_x(lambda x: xsend.at[k, lax.rem(x, 2)], xrecv.at[k], xs_sem.at[k], xr_sem.at[k])

    def collect(k):
        drain(xrecv.at[k], xr_sem.at[k])
        for x in range(NX):
            for b in range(FB):
                lhs[k, x * TOK : (x + 1) * TOK, b * LANES : (b + 1) * LANES] = xrecv[
                    k, x, b * TOK : (b + 1) * TOK, :
                ]

    def product(k, m):
        return jnp.dot(lhs[k], wbuf[m, k % 2], preferred_element_type=F32)

    def hand_over(m):
        for j in range(2):
            part_out[m, j] = part[m, :, j * QUART : (j + 1) * QUART].astype(BF16)
            send(
                part_out.at[m, j], part_in.at[m, my_h], ps_sem.at[m], pr_sem.at[m],
                place(my_y, 2 * j + 1 - my_k),
            )

    def whole(m):
        drain(part_in.at[m], pr_sem.at[m])
        return part[m] + jnp.concatenate([part_in[m, 0], part_in[m, 1]], axis=1).astype(F32)

    dispatch(0, p_exp)
    dispatch(1, p_exp)
    forward(0)
    dispatch(2, p_expw)
    forward(1)
    dispatch(3, p_expw)
    for m in range(3):
        kept[m].wait()
        drain(wbuf.at[m, core, :, pl.ds(other, QUART)], wb_sem.at[m])
        twins[m].start()
    forward(2)
    for m in range(3):
        twins[m].wait_recv()
    collect(0)
    for m in range(2):
        part[m] = product(0, m)
    collect(1)
    for m in range(2):
        part[m] += product(1, m)
        hand_over(m)
    forward(3)
    collect(2)
    part[2] = product(2, 2)
    collect(3)
    part[2] += product(3, 2)
    hand_over(2)

    pre_gate = whole(0)
    pre_up = whole(1)
    sig = jax.nn.sigmoid(pre_gate)
    gate_factor = pre_up * sig * (1.0 + pre_gate * (1.0 - sig))
    up_factor = pre_gate * sig
    grad_hid = whole(2)
    d_gate = (grad_hid * gate_factor).astype(BF16)
    d_up = (grad_hid * up_factor).astype(BF16)
    dims = (((1,), (1,)), ((), ()))
    for s in range(2):
        contrib = lax.dot_general(d_gate, wbuf[0, s], dims, preferred_element_type=F32)
        contrib = contrib + lax.dot_general(d_up, wbuf[1, s], dims, preferred_element_type=F32)
        contrib = contrib.astype(BF16)
        for x in range(NX):
            for b in range(FB):
                rsend[s, x, b * TOK : (b + 1) * TOK, :] = contrib[
                    x * TOK : (x + 1) * TOK, b * LANES : (b + 1) * LANES
                ]
        start_x(lambda x: rsend.at[s, x], rrecv.at[s], rs_sem.at[s], rr_sem.at[s])

    for s in range(2):
        drain(rrecv.at[s], rr_sem.at[s])
        summed = [(rrecv[s, f].astype(F32) + rrecv[s, f + 2].astype(F32)).astype(BF16) for f in range(2)]
        qsend[s] = reorder(p_mat_t[...], jnp.concatenate(summed, axis=0)).reshape(NY, BLK * CAP_E, LANES)
        start_y(qsend.at[s], qrecv.at[s], qs_sem.at[s], qr_sem.at[s])
    for s in range(2):
        drain(qrecv.at[s], qr_sem.at[s])
        bsend[s] = reorder(p_exp_t[...], qrecv[s].reshape(ROWS, LANES)).reshape(NZ, BLK * CAP_G, LANES)
        start_z(bsend.at[s], brecv.at[s], bs_sem.at[s], br_sem.at[s])
    for s in range(2):
        drain(brecv.at[s], br_sem.at[s])
        result = reorder(p_grp_t[...], brecv[s].reshape(ROWS, LANES))
        for k, (f, b) in enumerate(blocks()):
            out_ref[:, feature(f, s, b)] = result[k * TOK : (k + 1) * TOK, :]

    for k in range(4):
        drain(zsend.at[k, pl.ds(0, NZ - 1)], zs_sem.at[k])
        drain(ysend.at[k, pl.ds(0, NY - 1)], ys_sem.at[k])
        drain(xrecv.at[k, pl.ds(0, NX - 1)], xs_sem.at[k])
    for s in range(2):
        drain(rsend.at[s, pl.ds(0, NX - 1)], rs_sem.at[s])
        drain(qsend.at[s, pl.ds(0, NY - 1)], qs_sem.at[s])
        drain(bsend.at[s, pl.ds(0, NZ - 1)], bs_sem.at[s])
    for m in range(3):
        drain(part_out.at[m], ps_sem.at[m])
        twins[m].wait_send()

        @pl.when(my_k == 1)
        def _():
            swapped[m].wait_send()


def per_device(inputs_x, grad_out, group_order, route_picks, gate_weights, w_gate, w_up, w_down):
    hbm = pl.BlockSpec(memory_space=pltpu.HBM)
    square = pltpu.VMEM((ROWS, ROWS), BF16)
    dma = pltpu.SemaphoreType.DMA
    z_buf, y_buf, x_buf = (NZ, BLK * CAP_G, LANES), (NY, BLK * CAP_E, LANES), (NX, FB * TOK, LANES)
    return pl.pallas_call(
        kernel,
        out_shape=jax.ShapeDtypeStruct(inputs_x.shape, BF16),
        in_specs=[hbm] * 8,
        out_specs=pl.BlockSpec(memory_space=pltpu.VMEM),
        scratch_shapes=[
            pltpu.VMEM((1, NZ), I32),
            pltpu.VMEM((1, TOK), I32),
            pltpu.VMEM((1, TOK), BF16),
            pltpu.VMEM((2, TOK, 4 * HALF), BF16),
            pltpu.VMEM((2, ROWS, 2 * LANES), BF16),
            pltpu.VMEM((4, *z_buf), BF16),
            pltpu.VMEM((4, *z_buf), BF16),
            pltpu.VMEM((4, *y_buf), BF16),
            pltpu.VMEM((4, *y_buf), BF16),
            pltpu.VMEM((4, 2, FB * TOK, LANES), BF16),
            pltpu.VMEM((4, *x_buf), BF16),
            pltpu.VMEM((4, NX * TOK, HALF), BF16),
            pltpu.VMEM((3, 2, HALF, HALF), BF16),
            pltpu.VMEM((3, NX * TOK, HALF), F32),
            pltpu.VMEM((3, 2, NX * TOK, QUART), BF16),
            pltpu.VMEM((3, 2, NX * TOK, QUART), BF16),
            pltpu.VMEM((2, *x_buf), BF16),
            pltpu.VMEM((2, *x_buf), BF16),
            pltpu.VMEM((2, *y_buf), BF16),
            pltpu.VMEM((2, *y_buf), BF16),
            pltpu.VMEM((2, *z_buf), BF16),
            pltpu.VMEM((2, *z_buf), BF16),
            square, square, square, square, square, square, square,
            dma((5,)), dma((3,)), dma((3,)), dma((3,)), dma((3,)), dma((3,)),
            dma((4,)), dma((4,)), dma((4,)), dma((4,)), dma((4,)), dma((4,)),
            dma((3,)), dma((3,)), dma((2,)), dma((2,)), dma((2,)), dma((2,)), dma((2,)), dma((2,)),
        ],
        compiler_params=pltpu.CompilerParams(
            collective_id=0, has_side_effects=True, vmem_limit_bytes=60 * 2**20
        ),
    )(
        group_order, route_picks.reshape(1, TOK), gate_weights.reshape(1, TOK), inputs_x, grad_out,
        w_gate, w_up, w_down,
    )


def solution(mesh):
    placed = P(("node", "local"), None)
    return jax.shard_map(
        per_device, mesh=mesh, in_specs=(placed,) * 8, out_specs=placed, check_vma=False
    )
```

```python
import jax
import jax.numpy as jnp
from jax import lax
from jax.experimental import pallas as pl
from jax.experimental.pallas import tpu as pltpu
from jax.sharding import PartitionSpec as P

MESH = pl.DeviceIdType.MESH
BF16 = jnp.bfloat16
F32 = jnp.float32
I32 = jnp.int32

NZ, NY, NX = 12, 8, 4
TOK = 48
CAP_G, CAP_E = 4, 6
LANES = 128
BLK = 8
FB = 4
ROWS = TOK * BLK
HALF = 512
QUART = 256


def one_hot(key):
    rows = lax.broadcasted_iota(I32, (ROWS, ROWS), 0)
    return jnp.where(rows == key, 1.0, 0.0).astype(BF16)


def reorder(matrix, value):
    return jnp.dot(matrix, value, preferred_element_type=F32).astype(BF16)


def column(row, size):
    shape = (size, row.shape[1])
    diag = lax.broadcasted_iota(I32, shape, 0) == lax.broadcasted_iota(I32, shape, 1)
    return jnp.sum(jnp.where(diag, row, 0.0), axis=1, keepdims=True)


def spread(values, index):
    shape = (values.shape[0], index.shape[1])
    hit = lax.broadcasted_iota(I32, shape, 0) == index
    return jnp.sum(jnp.where(hit, values, 0.0), axis=0, keepdims=True)


def drain(ref, sem):
    pltpu.make_async_copy(ref, ref, sem).wait()


def kernel(
    order_hbm, picks_hbm, gates_hbm, x_hbm, y_hbm, wg_hbm, wu_hbm, wd_hbm, out_ref,
    order_ref, picks_ref, gates_ref, rows_in, stage, zsend, zrecv, ysend, yrecv, xsend, xrecv, lhs,
    wbuf, part, part_out, part_in, rsend, rrecv, qsend, qrecv, bsend, brecv,
    p_grp, p_exp, p_expw, p_mat, p_mat_t, p_exp_t, p_grp_t,
    in_sem, wa_sem, wb_sem, wo_sem, ws_sem, wr_sem, zs_sem, zr_sem, ys_sem, yr_sem, xs_sem, xr_sem,
    ps_sem, pr_sem, rs_sem, rr_sem, qs_sem, qr_sem, bs_sem, br_sem,
):
    node = lax.axis_index("node")
    local = lax.axis_index("local")
    core = lax.rem(local, 2)
    my_x = lax.rem(lax.div(local, 2), NX)
    my_y = lax.div(local, 2 * NX)
    my_h, my_k = lax.div(my_x, 2), lax.rem(my_x, 2)

    def place(y, x):
        return (node, (y * NX + x) * 2 + core)

    z_peers = [lax.rem(node + step, NZ) for step in (6, 5, 7, 4, 8, 3, 9, 2, 10, 1, 11)]
    y_peers = [lax.rem(my_y + step, NY) for step in (4, 3, 5, 2, 6, 1, 7)]
    x_peers = [lax.rem(my_x + step, NX) for step in (2, 1, 3)]
    twin = (node, local + 1 - 2 * core)

    barrier = pltpu.get_barrier_semaphore()

    def greet(device):
        pl.semaphore_signal(barrier, inc=1, device_id=device, device_id_type=MESH)

    for z in z_peers:
        greet((z, local))
    for y in y_peers:
        greet(place(y, my_x))
    for x in x_peers:
        greet(place(my_y, x))
    greet(twin)

    load_x = pltpu.make_async_copy(x_hbm, rows_in.at[0], in_sem.at[0])
    load_y = pltpu.make_async_copy(y_hbm, rows_in.at[1], in_sem.at[1])
    small = [
        pltpu.make_async_copy(src, dst, in_sem.at[2 + i])
        for i, (src, dst) in enumerate(
            ((order_hbm, order_ref), (picks_hbm, picks_ref), (gates_hbm, gates_ref))
        )
    ]
    small[0].start()
    load_x.start()
    load_y.start()
    small[1].start()
    small[2].start()

    lane = lax.broadcasted_iota(I32, (1, ROWS), 1)
    tok_k, tok_t = lax.div(lane, TOK), lax.rem(lane, TOK)
    small[0].wait()
    order = column(order_ref[...].astype(F32), 16)
    group = spread(order, lax.rem(tok_t, NZ)).astype(I32)
    p_grp[...] = one_hot(group * (BLK * CAP_G) + tok_k * CAP_G + lax.div(tok_t, NZ))

    def feature(f, s, b):
        start = f * 2 * HALF + s * HALF + b * LANES
        return slice(start, start + LANES)

    def blocks():
        return [(f, b) for f in range(2) for b in range(FB)]

    def pack(arr):
        for k, (f, b) in enumerate(blocks()):
            for s in range(2):
                stage[arr, k * TOK : (k + 1) * TOK, s * LANES : (s + 1) * LANES] = rows_in[
                    arr, :, feature(f, s, b)
                ]
        packed = reorder(p_grp[...], stage[arr])
        for s in range(2):
            zsend[2 * arr + s] = packed[:, s * LANES : (s + 1) * LANES].reshape(NZ, BLK * CAP_G, LANES)

    def send(src, dst, s_sem, r_sem, device):
        pltpu.make_async_remote_copy(
            src_ref=src, dst_ref=dst, send_sem=s_sem, recv_sem=r_sem, device_id=device, device_id_type=MESH
        ).start()

    def start_z(src, dst, s_sem, r_sem):
        for z in z_peers:
            send(src.at[z], dst.at[node], s_sem, r_sem, (z, local))
        pltpu.make_async_copy(src.at[node], dst.at[node], r_sem).start()

    def start_y(src, dst, s_sem, r_sem):
        for y in y_peers:
            send(src.at[y], dst.at[my_y], s_sem, r_sem, place(y, my_x))
        pltpu.make_async_copy(src.at[my_y], dst.at[my_y], r_sem).start()

    def start_x(src_of, dst, s_sem, r_sem):
        for x in x_peers:
            send(src_of(x), dst.at[my_x], s_sem, r_sem, place(my_y, x))
        pltpu.make_async_copy(src_of(my_x), dst.at[my_x], r_sem).start()

    load_x.wait()
    pack(0)
    load_y.wait()
    pack(1)
    pl.semaphore_wait(barrier, NZ - 1 + NY - 1 + NX - 1 + 1)
    for z in z_peers:
        send(zsend.at[pl.ds(0, 2), z], zrecv.at[pl.ds(0, 2), node], zs_sem.at[0], zr_sem.at[0], (z, local))
    pltpu.make_async_copy(zsend.at[pl.ds(0, 2), node], zrecv.at[pl.ds(0, 2), node], zr_sem.at[0]).start()
    for k in range(2, 4):
        start_z(zsend.at[k], zrecv.at[k], zs_sem.at[k], zr_sem.at[k])

    keep = pl.multiple_of(my_h * QUART, QUART)
    other = pl.multiple_of(QUART - my_h * QUART, QUART)
    weights = (wg_hbm, wu_hbm, wd_hbm)
    kept = [
        pltpu.make_async_copy(
            w.at[:, pl.ds(keep, QUART)], wbuf.at[m, core, :, pl.ds(keep, QUART)], wa_sem.at[m]
        )
        for m, w in enumerate(weights)
    ]
    swapped = [
        pltpu.make_async_remote_copy(
            src_ref=w.at[:, pl.ds(other, QUART)], dst_ref=wbuf.at[m, core, :, pl.ds(keep, QUART)],
            send_sem=wo_sem.at[m], recv_sem=wb_sem.at[m],
            device_id=place(my_y, lax.rem(my_x + 2, NX)), device_id_type=MESH,
        )
        for m, w in enumerate(weights)
    ]
    for m, w in enumerate(weights):
        kept[m].start()

        @pl.when(my_k == 0)
        def _():
            pltpu.make_async_copy(
                w.at[:, pl.ds(other, QUART)], wbuf.at[m, core, :, pl.ds(other, QUART)], wb_sem.at[m]
            ).start()

        @pl.when(my_k == 1)
        def _():
            swapped[m].start()

    twins = [
        pltpu.make_async_remote_copy(
            src_ref=wbuf.at[m, core], dst_ref=wbuf.at[m, core], send_sem=ws_sem.at[m], recv_sem=wr_sem.at[m],
            device_id=twin, device_id_type=MESH,
        )
        for m in range(3)
    ]

    small[1].wait()
    small[2].wait()
    picks_lane = picks_ref[...].astype(F32)
    picks = column(picks_lane, TOK)
    row48 = lax.broadcasted_iota(I32, (TOK, TOK), 0)
    col48 = lax.broadcasted_iota(I32, (TOK, TOK), 1)
    same = (picks == picks_lane) & (col48 < row48)
    rank = jnp.sum(jnp.where(same, 1.0, 0.0), axis=1, keepdims=True)
    grp_n, grp_k, grp_c = lax.div(lane, BLK * CAP_G), lax.rem(lax.div(lane, CAP_G), BLK), lax.rem(lane, CAP_G)
    grp_row = grp_n * CAP_G + grp_c
    slot_key = spread(picks * (BLK * CAP_E) + rank, grp_row).astype(I32) + grp_k * CAP_E
    gate = spread(column(gates_ref[...].astype(F32), TOK), grp_row)
    p_exp[...] = one_hot(slot_key)
    rows2d = lax.broadcasted_iota(I32, (ROWS, ROWS), 0)
    p_expw[...] = jnp.where(rows2d == slot_key, gate, 0.0).astype(BF16)
    exp_e, exp_k, exp_r = (
        lax.div(lane, BLK * CAP_E), lax.rem(lax.div(lane, CAP_E), BLK), lax.rem(lane, CAP_E),
    )
    p_mat[...] = one_hot(exp_k * TOK + exp_e * CAP_E + exp_r)
    mat_k, mat_y, mat_r = (
        lax.div(lane, TOK), lax.div(lax.rem(lane, TOK), CAP_E), lax.rem(lane, CAP_E),
    )
    p_mat_t[...] = one_hot(mat_y * (BLK * CAP_E) + mat_k * CAP_E + mat_r)
    row_id = lax.broadcasted_iota(I32, (TOK, ROWS), 0).astype(F32)
    wanted = (exp_e * CAP_E + exp_r).astype(F32)
    source = jnp.sum(
        jnp.where(picks * CAP_E + rank == wanted, row_id, 0.0), axis=0, keepdims=True
    ).astype(I32)
    p_exp_t[...] = one_hot(
        lax.div(source, CAP_G) * (BLK * CAP_G) + exp_k * CAP_G + lax.rem(source, CAP_G)
    )
    turn_id = lax.broadcasted_iota(I32, (16, ROWS), 0)
    at_group = (order == grp_n.astype(F32)) & (turn_id < NZ)
    position = jnp.sum(
        jnp.where(at_group, turn_id.astype(F32), 0.0), axis=0, keepdims=True
    ).astype(I32)
    p_grp_t[...] = one_hot(grp_k * TOK + grp_c * NZ + position)

    def dispatch(k, matrix):
        if k > 1:
            drain(zrecv.at[k], zr_sem.at[k])
        ysend[k] = reorder(matrix[...], zrecv[k].reshape(ROWS, LANES)).reshape(NY, BLK * CAP_E, LANES)
        start_y(ysend.at[k], yrecv.at[k], ys_sem.at[k], yr_sem.at[k])

    def forward(k):
        drain(yrecv.at[k], yr_sem.at[k])
        xsend[k] = reorder(p_mat[...], yrecv[k].reshape(ROWS, LANES)).reshape(2, FB * TOK, LANES)
        start_x(lambda x: xsend.at[k, lax.rem(x, 2)], xrecv.at[k], xs_sem.at[k], xr_sem.at[k])

    def collect(k):
        drain(xrecv.at[k], xr_sem.at[k])
        for x in range(NX):
            for b in range(FB):
                lhs[k, x * TOK : (x + 1) * TOK, b * LANES : (b + 1) * LANES] = xrecv[
                    k, x, b * TOK : (b + 1) * TOK, :
                ]

    def product(k, m):
        return jnp.dot(lhs[k], wbuf[m, k % 2], preferred_element_type=F32)

    def hand_over(m):
        for j in range(2):
            part_out[m, j] = part[m, :, j * QUART : (j + 1) * QUART].astype(BF16)
            send(
                part_out.at[m, j], part_in.at[m, my_h], ps_sem.at[m], pr_sem.at[m],
                place(my_y, 2 * j + 1 - my_k),
            )

    def whole(m):
        drain(part_in.at[m], pr_sem.at[m])
        return part[m] + jnp.concatenate([part_in[m, 0], part_in[m, 1]], axis=1).astype(F32)

    drain(zrecv.at[pl.ds(0, 2)], zr_sem.at[0])
    dispatch(0, p_exp)
    dispatch(1, p_exp)
    forward(0)
    dispatch(2, p_expw)
    forward(1)
    dispatch(3, p_expw)
    for m in range(3):
        kept[m].wait()
        drain(wbuf.at[m, core, :, pl.ds(other, QUART)], wb_sem.at[m])
        twins[m].start()
    forward(2)
    for m in range(3):
        twins[m].wait_recv()
    collect(0)
    for m in range(2):
        part[m] = product(0, m)
    collect(1)
    part[0] += product(1, 0)
    hand_over(0)
    forward(3)
    part[1] += product(1, 1)
    hand_over(1)
    collect(2)
    part[2] = product(2, 2)
    collect(3)
    part[2] += product(3, 2)
    hand_over(2)

    pre_gate = whole(0)
    pre_up = whole(1)
    sig = jax.nn.sigmoid(pre_gate)
    gate_factor = pre_up * sig * (1.0 + pre_gate * (1.0 - sig))
    up_factor = pre_gate * sig
    grad_hid = whole(2)
    d_gate = (grad_hid * gate_factor).astype(BF16)
    d_up = (grad_hid * up_factor).astype(BF16)
    dims = (((1,), (1,)), ((), ()))
    for s in range(2):
        contrib = lax.dot_general(d_gate, wbuf[0, s], dims, preferred_element_type=F32)
        contrib = contrib + lax.dot_general(d_up, wbuf[1, s], dims, preferred_element_type=F32)
        contrib = contrib.astype(BF16)
        for x in range(NX):
            for b in range(FB):
                rsend[s, x, b * TOK : (b + 1) * TOK, :] = contrib[
                    x * TOK : (x + 1) * TOK, b * LANES : (b + 1) * LANES
                ]
        start_x(lambda x: rsend.at[s, x], rrecv.at[s], rs_sem.at[s], rr_sem.at[s])

    for s in range(2):
        drain(rrecv.at[s], rr_sem.at[s])
        summed = [(rrecv[s, f].astype(F32) + rrecv[s, f + 2].astype(F32)).astype(BF16) for f in range(2)]
        qsend[s] = reorder(p_mat_t[...], jnp.concatenate(summed, axis=0)).reshape(NY, BLK * CAP_E, LANES)
        start_y(qsend.at[s], qrecv.at[s], qs_sem.at[s], qr_sem.at[s])
    for s in range(2):
        drain(qrecv.at[s], qr_sem.at[s])
        bsend[s] = reorder(p_exp_t[...], qrecv[s].reshape(ROWS, LANES)).reshape(NZ, BLK * CAP_G, LANES)
        start_z(bsend.at[s], brecv.at[s], bs_sem.at[s], br_sem.at[s])
    for s in range(2):
        drain(brecv.at[s], br_sem.at[s])
        result = reorder(p_grp_t[...], brecv[s].reshape(ROWS, LANES))
        for k, (f, b) in enumerate(blocks()):
            out_ref[:, feature(f, s, b)] = result[k * TOK : (k + 1) * TOK, :]

    drain(zsend.at[pl.ds(0, 2), pl.ds(0, NZ - 1)], zs_sem.at[0])
    for k in range(4):
        if k > 1:
            drain(zsend.at[k, pl.ds(0, NZ - 1)], zs_sem.at[k])
        drain(ysend.at[k, pl.ds(0, NY - 1)], ys_sem.at[k])
        drain(xrecv.at[k, pl.ds(0, NX - 1)], xs_sem.at[k])
    for s in range(2):
        drain(rsend.at[s, pl.ds(0, NX - 1)], rs_sem.at[s])
        drain(qsend.at[s, pl.ds(0, NY - 1)], qs_sem.at[s])
        drain(bsend.at[s, pl.ds(0, NZ - 1)], bs_sem.at[s])
    for m in range(3):
        drain(part_out.at[m], ps_sem.at[m])
        twins[m].wait_send()

        @pl.when(my_k == 1)
        def _():
            swapped[m].wait_send()


def per_device(inputs_x, grad_out, group_order, route_picks, gate_weights, w_gate, w_up, w_down):
    hbm = pl.BlockSpec(memory_space=pltpu.HBM)
    square = pltpu.VMEM((ROWS, ROWS), BF16)
    dma = pltpu.SemaphoreType.DMA
    z_buf, y_buf, x_buf = (NZ, BLK * CAP_G, LANES), (NY, BLK * CAP_E, LANES), (NX, FB * TOK, LANES)
    return pl.pallas_call(
        kernel,
        out_shape=jax.ShapeDtypeStruct(inputs_x.shape, BF16),
        in_specs=[hbm] * 8,
        out_specs=pl.BlockSpec(memory_space=pltpu.VMEM),
        scratch_shapes=[
            pltpu.VMEM((1, NZ), I32),
            pltpu.VMEM((1, TOK), I32),
            pltpu.VMEM((1, TOK), BF16),
            pltpu.VMEM((2, TOK, 4 * HALF), BF16),
            pltpu.VMEM((2, ROWS, 2 * LANES), BF16),
            pltpu.VMEM((4, *z_buf), BF16),
            pltpu.VMEM((4, *z_buf), BF16),
            pltpu.VMEM((4, *y_buf), BF16),
            pltpu.VMEM((4, *y_buf), BF16),
            pltpu.VMEM((4, 2, FB * TOK, LANES), BF16),
            pltpu.VMEM((4, *x_buf), BF16),
            pltpu.VMEM((4, NX * TOK, HALF), BF16),
            pltpu.VMEM((3, 2, HALF, HALF), BF16),
            pltpu.VMEM((3, NX * TOK, HALF), F32),
            pltpu.VMEM((3, 2, NX * TOK, QUART), BF16),
            pltpu.VMEM((3, 2, NX * TOK, QUART), BF16),
            pltpu.VMEM((2, *x_buf), BF16),
            pltpu.VMEM((2, *x_buf), BF16),
            pltpu.VMEM((2, *y_buf), BF16),
            pltpu.VMEM((2, *y_buf), BF16),
            pltpu.VMEM((2, *z_buf), BF16),
            pltpu.VMEM((2, *z_buf), BF16),
            square, square, square, square, square, square, square,
            dma((5,)), dma((3,)), dma((3,)), dma((3,)), dma((3,)), dma((3,)),
            dma((4,)), dma((4,)), dma((4,)), dma((4,)), dma((4,)), dma((4,)),
            dma((3,)), dma((3,)), dma((2,)), dma((2,)), dma((2,)), dma((2,)), dma((2,)), dma((2,)),
        ],
        compiler_params=pltpu.CompilerParams(
            collective_id=0, has_side_effects=True, vmem_limit_bytes=60 * 2**20
        ),
    )(
        group_order, route_picks.reshape(1, TOK), gate_weights.reshape(1, TOK), inputs_x, grad_out,
        w_gate, w_up, w_down,
    )


def solution(mesh):
    placed = P(("node", "local"), None)
    return jax.shard_map(
        per_device, mesh=mesh, in_specs=(placed,) * 8, out_specs=placed, check_vma=False
    )
```

```python
import jax
import jax.numpy as jnp
from jax import lax
from jax.experimental import pallas as pl
from jax.experimental.pallas import tpu as pltpu
from jax.sharding import PartitionSpec as P

MESH = pl.DeviceIdType.MESH
BF16 = jnp.bfloat16
F32 = jnp.float32
I32 = jnp.int32

NZ, NY, NX = 12, 8, 4
TOK = 48
CAP_G, CAP_E = 4, 6
LANES = 128
BLK = 8
FB = 4
ROWS = TOK * BLK
HALF = 512
QUART = 256


def one_hot(key):
    rows = lax.broadcasted_iota(I32, (ROWS, ROWS), 0)
    return jnp.where(rows == key, 1.0, 0.0).astype(BF16)


def reorder(matrix, value):
    return jnp.dot(matrix, value, preferred_element_type=F32).astype(BF16)


def column(row, size):
    shape = (size, row.shape[1])
    diag = lax.broadcasted_iota(I32, shape, 0) == lax.broadcasted_iota(I32, shape, 1)
    return jnp.sum(jnp.where(diag, row, 0.0), axis=1, keepdims=True)


def spread(values, index):
    shape = (values.shape[0], index.shape[1])
    hit = lax.broadcasted_iota(I32, shape, 0) == index
    return jnp.sum(jnp.where(hit, values, 0.0), axis=0, keepdims=True)


def drain(ref, sem):
    pltpu.make_async_copy(ref, ref, sem).wait()


def kernel(
    order_hbm, picks_hbm, gates_hbm, x_hbm, y_hbm, wg_hbm, wu_hbm, wd_hbm, out_ref,
    order_ref, picks_ref, gates_ref, rows_in, stage, zsend, zrecv, ysend, yrecv, xsend, xrecv, lhs,
    wbuf, part, part_out, part_in, rsend, rrecv, qsend, qrecv, bsend, brecv,
    p_grp, p_exp, p_expw, p_mat, p_mat_t, p_exp_t, p_grp_t,
    in_sem, wa_sem, wb_sem, wo_sem, ws_sem, wr_sem, zs_sem, zr_sem, ys_sem, yr_sem, xs_sem, xr_sem,
    ps_sem, pr_sem, rs_sem, rr_sem, qs_sem, qr_sem, bs_sem, br_sem,
):
    node = lax.axis_index("node")
    local = lax.axis_index("local")
    core = lax.rem(local, 2)
    my_x = lax.rem(lax.div(local, 2), NX)
    my_y = lax.div(local, 2 * NX)
    my_h, my_k = lax.div(my_x, 2), lax.rem(my_x, 2)

    def place(y, x):
        return (node, (y * NX + x) * 2 + core)

    z_peers = [lax.rem(node + step, NZ) for step in (6, 5, 7, 4, 8, 3, 9, 2, 10, 1, 11)]
    y_peers = [lax.rem(my_y + step, NY) for step in (4, 3, 5, 2, 6, 1, 7)]
    x_peers = [lax.rem(my_x + step, NX) for step in (2, 1, 3)]
    twin = (node, local + 1 - 2 * core)

    barrier = pltpu.get_barrier_semaphore()

    def greet(device):
        pl.semaphore_signal(barrier, inc=1, device_id=device, device_id_type=MESH)

    for z in z_peers:
        greet((z, local))
    for y in y_peers:
        greet(place(y, my_x))
    for x in x_peers:
        greet(place(my_y, x))
    greet(twin)

    load_x = pltpu.make_async_copy(x_hbm, rows_in.at[0], in_sem.at[0])
    load_y = pltpu.make_async_copy(y_hbm, rows_in.at[1], in_sem.at[1])
    small = [
        pltpu.make_async_copy(src, dst, in_sem.at[2 + i])
        for i, (src, dst) in enumerate(
            ((order_hbm, order_ref), (picks_hbm, picks_ref), (gates_hbm, gates_ref))
        )
    ]
    small[0].start()
    load_x.start()
    load_y.start()
    small[1].start()
    small[2].start()

    lane = lax.broadcasted_iota(I32, (1, ROWS), 1)
    tok_k, tok_t = lax.div(lane, TOK), lax.rem(lane, TOK)
    small[0].wait()
    order = column(order_ref[...].astype(F32), 16)
    group = spread(order, lax.rem(tok_t, NZ)).astype(I32)
    p_grp[...] = one_hot(group * (BLK * CAP_G) + tok_k * CAP_G + lax.div(tok_t, NZ))

    def feature(f, s, b):
        start = f * 2 * HALF + s * HALF + b * LANES
        return slice(start, start + LANES)

    def blocks():
        return [(f, b) for f in range(2) for b in range(FB)]

    def pack(arr):
        for k, (f, b) in enumerate(blocks()):
            for s in range(2):
                stage[arr, k * TOK : (k + 1) * TOK, s * LANES : (s + 1) * LANES] = rows_in[
                    arr, :, feature(f, s, b)
                ]
        packed = reorder(p_grp[...], stage[arr])
        for s in range(2):
            zsend[2 * arr + s] = packed[:, s * LANES : (s + 1) * LANES].reshape(NZ, BLK * CAP_G, LANES)

    def send(src, dst, s_sem, r_sem, device):
        pltpu.make_async_remote_copy(
            src_ref=src, dst_ref=dst, send_sem=s_sem, recv_sem=r_sem, device_id=device, device_id_type=MESH
        ).start()

    def start_z(src, dst, s_sem, r_sem):
        for z in z_peers:
            send(src.at[z], dst.at[node], s_sem, r_sem, (z, local))
        pltpu.make_async_copy(src.at[node], dst.at[node], r_sem).start()

    def start_y(src, dst, s_sem, r_sem):
        for y in y_peers:
            send(src.at[y], dst.at[my_y], s_sem, r_sem, place(y, my_x))
        pltpu.make_async_copy(src.at[my_y], dst.at[my_y], r_sem).start()

    def start_x(src_of, dst, s_sem, r_sem):
        for x in x_peers:
            send(src_of(x), dst.at[my_x], s_sem, r_sem, place(my_y, x))
        pltpu.make_async_copy(src_of(my_x), dst.at[my_x], r_sem).start()

    load_x.wait()
    pack(0)
    load_y.wait()
    pack(1)
    pl.semaphore_wait(barrier, NZ - 1 + NY - 1 + NX - 1 + 1)
    for z in z_peers:
        send(zsend.at[pl.ds(0, 2), z], zrecv.at[pl.ds(0, 2), node], zs_sem.at[0], zr_sem.at[0], (z, local))
    pltpu.make_async_copy(zsend.at[pl.ds(0, 2), node], zrecv.at[pl.ds(0, 2), node], zr_sem.at[0]).start()
    for k in range(2, 4):
        start_z(zsend.at[k], zrecv.at[k], zs_sem.at[k], zr_sem.at[k])

    keep = pl.multiple_of(my_h * QUART, QUART)
    other = pl.multiple_of(QUART - my_h * QUART, QUART)
    weights = (wg_hbm, wu_hbm, wd_hbm)
    kept = [
        pltpu.make_async_copy(
            w.at[:, pl.ds(keep, QUART)], wbuf.at[m, core, :, pl.ds(keep, QUART)], wa_sem.at[m]
        )
        for m, w in enumerate(weights)
    ]
    swapped = [
        pltpu.make_async_remote_copy(
            src_ref=w.at[:, pl.ds(other, QUART)], dst_ref=wbuf.at[m, core, :, pl.ds(keep, QUART)],
            send_sem=wo_sem.at[m], recv_sem=wb_sem.at[m],
            device_id=place(my_y, lax.rem(my_x + 2, NX)), device_id_type=MESH,
        )
        for m, w in enumerate(weights)
    ]
    for m, w in enumerate(weights):
        kept[m].start()

        @pl.when(my_k == 0)
        def _():
            pltpu.make_async_copy(
                w.at[:, pl.ds(other, QUART)], wbuf.at[m, core, :, pl.ds(other, QUART)], wb_sem.at[m]
            ).start()

        @pl.when(my_k == 1)
        def _():
            swapped[m].start()

    twins = [
        pltpu.make_async_remote_copy(
            src_ref=wbuf.at[m, core], dst_ref=wbuf.at[m, core], send_sem=ws_sem.at[m], recv_sem=wr_sem.at[m],
            device_id=twin, device_id_type=MESH,
        )
        for m in range(3)
    ]

    small[1].wait()
    small[2].wait()
    picks_lane = picks_ref[...].astype(F32)
    picks = column(picks_lane, TOK)
    row48 = lax.broadcasted_iota(I32, (TOK, TOK), 0)
    col48 = lax.broadcasted_iota(I32, (TOK, TOK), 1)
    same = (picks == picks_lane) & (col48 < row48)
    rank = jnp.sum(jnp.where(same, 1.0, 0.0), axis=1, keepdims=True)
    grp_n, grp_k, grp_c = lax.div(lane, BLK * CAP_G), lax.rem(lax.div(lane, CAP_G), BLK), lax.rem(lane, CAP_G)
    grp_row = grp_n * CAP_G + grp_c
    slot_key = spread(picks * (BLK * CAP_E) + rank, grp_row).astype(I32) + grp_k * CAP_E
    gate = spread(column(gates_ref[...].astype(F32), TOK), grp_row)
    p_exp[...] = one_hot(slot_key)
    rows2d = lax.broadcasted_iota(I32, (ROWS, ROWS), 0)
    p_expw[...] = jnp.where(rows2d == slot_key, gate, 0.0).astype(BF16)
    exp_e, exp_k, exp_r = (
        lax.div(lane, BLK * CAP_E), lax.rem(lax.div(lane, CAP_E), BLK), lax.rem(lane, CAP_E),
    )
    p_mat[...] = one_hot(exp_k * TOK + exp_e * CAP_E + exp_r)
    mat_k, mat_y, mat_r = (
        lax.div(lane, TOK), lax.div(lax.rem(lane, TOK), CAP_E), lax.rem(lane, CAP_E),
    )
    p_mat_t[...] = one_hot(mat_y * (BLK * CAP_E) + mat_k * CAP_E + mat_r)
    row_id = lax.broadcasted_iota(I32, (TOK, ROWS), 0).astype(F32)
    wanted = (exp_e * CAP_E + exp_r).astype(F32)
    source = jnp.sum(
        jnp.where(picks * CAP_E + rank == wanted, row_id, 0.0), axis=0, keepdims=True
    ).astype(I32)
    p_exp_t[...] = one_hot(
        lax.div(source, CAP_G) * (BLK * CAP_G) + exp_k * CAP_G + lax.rem(source, CAP_G)
    )
    turn_id = lax.broadcasted_iota(I32, (16, ROWS), 0)
    at_group = (order == grp_n.astype(F32)) & (turn_id < NZ)
    position = jnp.sum(
        jnp.where(at_group, turn_id.astype(F32), 0.0), axis=0, keepdims=True
    ).astype(I32)
    p_grp_t[...] = one_hot(grp_k * TOK + grp_c * NZ + position)

    def dispatch(k, matrix):
        if k > 1:
            drain(zrecv.at[k], zr_sem.at[k])
        ysend[k] = reorder(matrix[...], zrecv[k].reshape(ROWS, LANES)).reshape(NY, BLK * CAP_E, LANES)
        start_y(ysend.at[k], yrecv.at[k], ys_sem.at[k], yr_sem.at[k])

    def forward(k):
        drain(yrecv.at[k], yr_sem.at[k])
        xsend[k] = reorder(p_mat[...], yrecv[k].reshape(ROWS, LANES)).reshape(2, FB * TOK, LANES)
        start_x(lambda x: xsend.at[k, lax.rem(x, 2)], xrecv.at[k], xs_sem.at[k], xr_sem.at[k])

    def collect(k):
        drain(xrecv.at[k], xr_sem.at[k])
        for x in range(NX):
            for b in range(FB):
                lhs[k, x * TOK : (x + 1) * TOK, b * LANES : (b + 1) * LANES] = xrecv[
                    k, x, b * TOK : (b + 1) * TOK, :
                ]

    def product(k, m):
        return jnp.dot(lhs[k], wbuf[m, k % 2], preferred_element_type=F32)

    def hand_over(m):
        for j in range(2):
            part_out[m, j] = part[m, :, j * QUART : (j + 1) * QUART].astype(BF16)
            send(
                part_out.at[m, j], part_in.at[m, my_h], ps_sem.at[m], pr_sem.at[m],
                place(my_y, 2 * j + 1 - my_k),
            )

    def whole(m):
        drain(part_in.at[m], pr_sem.at[m])
        return part[m] + jnp.concatenate([part_in[m, 0], part_in[m, 1]], axis=1).astype(F32)

    drain(zrecv.at[pl.ds(0, 2)], zr_sem.at[0])
    dispatch(0, p_exp)
    dispatch(1, p_exp)
    forward(0)
    dispatch(2, p_expw)
    forward(1)
    dispatch(3, p_expw)
    for m in range(3):
        kept[m].wait()
        drain(wbuf.at[m, core, :, pl.ds(other, QUART)], wb_sem.at[m])
        twins[m].start()
    forward(2)
    for m in range(3):
        twins[m].wait_recv()
    collect(0)
    for m in range(2):
        part[m] = product(0, m)
    collect(1)
    part[0] += product(1, 0)
    hand_over(0)
    forward(3)
    part[1] += product(1, 1)
    hand_over(1)
    collect(2)
    part[2] = product(2, 2)
    collect(3)
    part[2] += product(3, 2)
    hand_over(2)

    pre_gate = whole(0)
    pre_up = whole(1)
    sig = jax.nn.sigmoid(pre_gate)
    gate_factor = pre_up * sig * (1.0 + pre_gate * (1.0 - sig))
    up_factor = pre_gate * sig
    grad_hid = whole(2)
    d_gate = (grad_hid * gate_factor).astype(BF16)
    d_up = (grad_hid * up_factor).astype(BF16)
    dims = (((1,), (1,)), ((), ()))
    for s in range(2):
        contrib = lax.dot_general(d_gate, wbuf[0, s], dims, preferred_element_type=F32)
        contrib = contrib + lax.dot_general(d_up, wbuf[1, s], dims, preferred_element_type=F32)
        contrib = contrib.astype(BF16)
        for x in range(NX):
            for b in range(FB):
                rsend[s, x, b * TOK : (b + 1) * TOK, :] = contrib[
                    x * TOK : (x + 1) * TOK, b * LANES : (b + 1) * LANES
                ]
        start_x(lambda x: rsend.at[s, x], rrecv.at[s], rs_sem.at[s], rr_sem.at[s])

    for s in range(2):
        drain(rrecv.at[s], rr_sem.at[s])
        summed = [(rrecv[s, f].astype(F32) + rrecv[s, f + 2].astype(F32)).astype(BF16) for f in range(2)]
        qsend[s] = reorder(p_mat_t[...], jnp.concatenate(summed, axis=0)).reshape(NY, BLK * CAP_E, LANES)
        start_y(qsend.at[s], qrecv.at[s], qs_sem.at[s], qr_sem.at[s])
    for s in range(2):
        drain(qrecv.at[s], qr_sem.at[s])
        bsend[s] = reorder(p_exp_t[...], qrecv[s].reshape(ROWS, LANES)).reshape(NZ, BLK * CAP_G, LANES)
        start_z(bsend.at[s], brecv.at[s], bs_sem.at[s], br_sem.at[s])
    drain(zsend.at[pl.ds(0, 2), pl.ds(0, NZ - 1)], zs_sem.at[0])
    for k in range(4):
        if k > 1:
            drain(zsend.at[k, pl.ds(0, NZ - 1)], zs_sem.at[k])
        drain(ysend.at[k, pl.ds(0, NY - 1)], ys_sem.at[k])
        drain(xrecv.at[k, pl.ds(0, NX - 1)], xs_sem.at[k])
    for s in range(2):
        drain(rsend.at[s, pl.ds(0, NX - 1)], rs_sem.at[s])
        drain(qsend.at[s, pl.ds(0, NY - 1)], qs_sem.at[s])
    for m in range(3):
        drain(part_out.at[m], ps_sem.at[m])
        twins[m].wait_send()

        @pl.when(my_k == 1)
        def _():
            swapped[m].wait_send()
    for s in range(2):
        drain(brecv.at[s], br_sem.at[s])
        result = reorder(p_grp_t[...], brecv[s].reshape(ROWS, LANES))
        for k, (f, b) in enumerate(blocks()):
            out_ref[:, feature(f, s, b)] = result[k * TOK : (k + 1) * TOK, :]
    for s in range(2):
        drain(bsend.at[s, pl.ds(0, NZ - 1)], bs_sem.at[s])


def per_device(inputs_x, grad_out, group_order, route_picks, gate_weights, w_gate, w_up, w_down):
    hbm = pl.BlockSpec(memory_space=pltpu.HBM)
    square = pltpu.VMEM((ROWS, ROWS), BF16)
    dma = pltpu.SemaphoreType.DMA
    z_buf, y_buf, x_buf = (NZ, BLK * CAP_G, LANES), (NY, BLK * CAP_E, LANES), (NX, FB * TOK, LANES)
    return pl.pallas_call(
        kernel,
        out_shape=jax.ShapeDtypeStruct(inputs_x.shape, BF16),
        in_specs=[hbm] * 8,
        out_specs=pl.BlockSpec(memory_space=pltpu.VMEM),
        scratch_shapes=[
            pltpu.VMEM((1, NZ), I32),
            pltpu.VMEM((1, TOK), I32),
            pltpu.VMEM((1, TOK), BF16),
            pltpu.VMEM((2, TOK, 4 * HALF), BF16),
            pltpu.VMEM((2, ROWS, 2 * LANES), BF16),
            pltpu.VMEM((4, *z_buf), BF16),
            pltpu.VMEM((4, *z_buf), BF16),
            pltpu.VMEM((4, *y_buf), BF16),
            pltpu.VMEM((4, *y_buf), BF16),
            pltpu.VMEM((4, 2, FB * TOK, LANES), BF16),
            pltpu.VMEM((4, *x_buf), BF16),
            pltpu.VMEM((4, NX * TOK, HALF), BF16),
            pltpu.VMEM((3, 2, HALF, HALF), BF16),
            pltpu.VMEM((3, NX * TOK, HALF), F32),
            pltpu.VMEM((3, 2, NX * TOK, QUART), BF16),
            pltpu.VMEM((3, 2, NX * TOK, QUART), BF16),
            pltpu.VMEM((2, *x_buf), BF16),
            pltpu.VMEM((2, *x_buf), BF16),
            pltpu.VMEM((2, *y_buf), BF16),
            pltpu.VMEM((2, *y_buf), BF16),
            pltpu.VMEM((2, *z_buf), BF16),
            pltpu.VMEM((2, *z_buf), BF16),
            square, square, square, square, square, square, square,
            dma((5,)), dma((3,)), dma((3,)), dma((3,)), dma((3,)), dma((3,)),
            dma((4,)), dma((4,)), dma((4,)), dma((4,)), dma((4,)), dma((4,)),
            dma((3,)), dma((3,)), dma((2,)), dma((2,)), dma((2,)), dma((2,)), dma((2,)), dma((2,)),
        ],
        compiler_params=pltpu.CompilerParams(
            collective_id=0, has_side_effects=True, vmem_limit_bytes=54886 * 2**10
        ),
    )(
        group_order, route_picks.reshape(1, TOK), gate_weights.reshape(1, TOK), inputs_x, grad_out,
        w_gate, w_up, w_down,
    )


def solution(mesh):
    placed = P(("node", "local"), None)
    return jax.shard_map(
        per_device, mesh=mesh, in_specs=(placed,) * 8, out_specs=placed, check_vma=False
    )
```

```python
import jax
import jax.numpy as jnp
from jax import lax
from jax.experimental import pallas as pl
from jax.experimental.pallas import tpu as pltpu
from jax.sharding import PartitionSpec as P

MESH = pl.DeviceIdType.MESH
BF16 = jnp.bfloat16
F32 = jnp.float32
I32 = jnp.int32

NZ, NY, NX = 12, 8, 4
TOK = 48
CAP_G, CAP_E = 4, 6
LANES = 128
BLK = 8
FB = 4
ROWS = TOK * BLK
HALF = 512
QUART = 256


def one_hot(key):
    rows = lax.broadcasted_iota(I32, (ROWS, ROWS), 0)
    return jnp.where(rows == key, 1.0, 0.0).astype(BF16)


def reorder(matrix, value):
    return jnp.dot(matrix, value, preferred_element_type=F32).astype(BF16)


def column(row, size):
    shape = (size, row.shape[1])
    diag = lax.broadcasted_iota(I32, shape, 0) == lax.broadcasted_iota(I32, shape, 1)
    return jnp.sum(jnp.where(diag, row, 0.0), axis=1, keepdims=True)


def spread(values, index):
    shape = (values.shape[0], index.shape[1])
    hit = lax.broadcasted_iota(I32, shape, 0) == index
    return jnp.sum(jnp.where(hit, values, 0.0), axis=0, keepdims=True)


def drain(ref, sem):
    pltpu.make_async_copy(ref, ref, sem).wait()


def kernel(
    order_hbm, picks_hbm, gates_hbm, x_hbm, y_hbm, wg_hbm, wu_hbm, wd_hbm, out_ref,
    order_ref, picks_ref, gates_ref, rows_in, stage, zsend, zrecv, ysend, yrecv, xsend, xrecv, lhs,
    wbuf, part, part_out, part_in, rsend, rrecv, qsend, qrecv, bsend, brecv,
    p_grp, p_exp, p_expw, p_mat, p_mat_t, p_exp_t, p_grp_t,
    in_sem, wa_sem, wb_sem, wo_sem, ws_sem, wr_sem, zs_sem, zr_sem, ys_sem, yr_sem, xs_sem, xr_sem,
    ps_sem, pr_sem, rs_sem, rr_sem, qs_sem, qr_sem, bs_sem, br_sem,
):
    node = lax.axis_index("node")
    local = lax.axis_index("local")
    core = lax.rem(local, 2)
    my_x = lax.rem(lax.div(local, 2), NX)
    my_y = lax.div(local, 2 * NX)
    my_h, my_k = lax.div(my_x, 2), lax.rem(my_x, 2)

    def place(y, x):
        return (node, (y * NX + x) * 2 + core)

    z_peers = [lax.rem(node + step, NZ) for step in (6, 5, 7, 4, 8, 3, 9, 2, 10, 1, 11)]
    y_peers = [lax.rem(my_y + step, NY) for step in (4, 3, 5, 2, 6, 1, 7)]
    x_peers = [lax.rem(my_x + step, NX) for step in (2, 1, 3)]
    twin = (node, local + 1 - 2 * core)

    barrier = pltpu.get_barrier_semaphore()

    def greet(device):
        pl.semaphore_signal(barrier, inc=1, device_id=device, device_id_type=MESH)

    for z in z_peers:
        greet((z, local))
    for y in y_peers:
        greet(place(y, my_x))
    for x in x_peers:
        greet(place(my_y, x))
    greet(twin)

    load_x = pltpu.make_async_copy(x_hbm, rows_in.at[0], in_sem.at[0])
    load_y = pltpu.make_async_copy(y_hbm, rows_in.at[1], in_sem.at[1])
    small = [
        pltpu.make_async_copy(src, dst, in_sem.at[2 + i])
        for i, (src, dst) in enumerate(
            ((order_hbm, order_ref), (picks_hbm, picks_ref), (gates_hbm, gates_ref))
        )
    ]
    small[0].start()
    load_x.start()
    load_y.start()
    small[1].start()
    small[2].start()

    lane = lax.broadcasted_iota(I32, (1, ROWS), 1)
    tok_k, tok_t = lax.div(lane, TOK), lax.rem(lane, TOK)
    small[0].wait()
    order = column(order_ref[...].astype(F32), 16)
    group = spread(order, lax.rem(tok_t, NZ)).astype(I32)
    p_grp[...] = one_hot(group * (BLK * CAP_G) + tok_k * CAP_G + lax.div(tok_t, NZ))

    def feature(f, s, b):
        start = f * 2 * HALF + s * HALF + b * LANES
        return slice(start, start + LANES)

    def blocks():
        return [(f, b) for f in range(2) for b in range(FB)]

    def pack(arr):
        for k, (f, b) in enumerate(blocks()):
            for s in range(2):
                stage[arr, k * TOK : (k + 1) * TOK, s * LANES : (s + 1) * LANES] = rows_in[
                    arr, :, feature(f, s, b)
                ]
        packed = reorder(p_grp[...], stage[arr])
        for s in range(2):
            zsend[2 * arr + s] = packed[:, s * LANES : (s + 1) * LANES].reshape(NZ, BLK * CAP_G, LANES)

    def send(src, dst, s_sem, r_sem, device):
        pltpu.make_async_remote_copy(
            src_ref=src, dst_ref=dst, send_sem=s_sem, recv_sem=r_sem, device_id=device, device_id_type=MESH
        ).start()

    def start_z(src, dst, s_sem, r_sem):
        for z in z_peers:
            send(src.at[z], dst.at[node], s_sem, r_sem, (z, local))
        pltpu.make_async_copy(src.at[node], dst.at[node], r_sem).start()

    def start_y(src, dst, s_sem, r_sem):
        for y in y_peers:
            send(src.at[y], dst.at[my_y], s_sem, r_sem, place(y, my_x))
        pltpu.make_async_copy(src.at[my_y], dst.at[my_y], r_sem).start()

    def start_x(src_of, dst, s_sem, r_sem):
        for x in x_peers:
            send(src_of(x), dst.at[my_x], s_sem, r_sem, place(my_y, x))
        pltpu.make_async_copy(src_of(my_x), dst.at[my_x], r_sem).start()

    load_x.wait()
    pack(0)
    load_y.wait()
    pack(1)
    pl.semaphore_wait(barrier, NZ - 1 + NY - 1 + NX - 1 + 1)
    for z in z_peers:
        send(zsend.at[pl.ds(0, 2), z], zrecv.at[pl.ds(0, 2), node], zs_sem.at[0], zr_sem.at[0], (z, local))
    pltpu.make_async_copy(zsend.at[pl.ds(0, 2), node], zrecv.at[pl.ds(0, 2), node], zr_sem.at[0]).start()
    for k in range(2, 4):
        start_z(zsend.at[k], zrecv.at[k], zs_sem.at[k], zr_sem.at[k])

    keep = pl.multiple_of(my_h * QUART, QUART)
    other = pl.multiple_of(QUART - my_h * QUART, QUART)
    weights = (wg_hbm, wu_hbm, wd_hbm)
    kept = [
        pltpu.make_async_copy(
            w.at[:, pl.ds(keep, QUART)], wbuf.at[m, core, :, pl.ds(keep, QUART)], wa_sem.at[m]
        )
        for m, w in enumerate(weights)
    ]
    swapped = [
        pltpu.make_async_remote_copy(
            src_ref=w.at[:, pl.ds(other, QUART)], dst_ref=wbuf.at[m, core, :, pl.ds(keep, QUART)],
            send_sem=wo_sem.at[m], recv_sem=wb_sem.at[m],
            device_id=place(my_y, lax.rem(my_x + 2, NX)), device_id_type=MESH,
        )
        for m, w in enumerate(weights)
    ]
    for m, w in enumerate(weights):
        kept[m].start()

        @pl.when(my_k == 0)
        def _():
            pltpu.make_async_copy(
                w.at[:, pl.ds(other, QUART)], wbuf.at[m, core, :, pl.ds(other, QUART)], wb_sem.at[m]
            ).start()

        @pl.when(my_k == 1)
        def _():
            swapped[m].start()

    twins = [
        pltpu.make_async_remote_copy(
            src_ref=wbuf.at[m, core], dst_ref=wbuf.at[m, core], send_sem=ws_sem.at[m], recv_sem=wr_sem.at[m],
            device_id=twin, device_id_type=MESH,
        )
        for m in range(3)
    ]

    small[1].wait()
    small[2].wait()
    picks_lane = picks_ref[...].astype(F32)
    picks = column(picks_lane, TOK)
    row48 = lax.broadcasted_iota(I32, (TOK, TOK), 0)
    col48 = lax.broadcasted_iota(I32, (TOK, TOK), 1)
    same = (picks == picks_lane) & (col48 < row48)
    rank = jnp.sum(jnp.where(same, 1.0, 0.0), axis=1, keepdims=True)
    grp_n, grp_k, grp_c = lax.div(lane, BLK * CAP_G), lax.rem(lax.div(lane, CAP_G), BLK), lax.rem(lane, CAP_G)
    grp_row = grp_n * CAP_G + grp_c
    slot_key = spread(picks * (BLK * CAP_E) + rank, grp_row).astype(I32) + grp_k * CAP_E
    gate = spread(column(gates_ref[...].astype(F32), TOK), grp_row)
    p_exp[...] = one_hot(slot_key)
    rows2d = lax.broadcasted_iota(I32, (ROWS, ROWS), 0)
    p_expw[...] = jnp.where(rows2d == slot_key, gate, 0.0).astype(BF16)
    exp_e, exp_k, exp_r = (
        lax.div(lane, BLK * CAP_E), lax.rem(lax.div(lane, CAP_E), BLK), lax.rem(lane, CAP_E),
    )
    p_mat[...] = one_hot(exp_k * TOK + exp_e * CAP_E + exp_r)
    mat_k, mat_y, mat_r = (
        lax.div(lane, TOK), lax.div(lax.rem(lane, TOK), CAP_E), lax.rem(lane, CAP_E),
    )
    p_mat_t[...] = one_hot(mat_y * (BLK * CAP_E) + mat_k * CAP_E + mat_r)
    row_id = lax.broadcasted_iota(I32, (TOK, ROWS), 0).astype(F32)
    wanted = (exp_e * CAP_E + exp_r).astype(F32)
    source = jnp.sum(
        jnp.where(picks * CAP_E + rank == wanted, row_id, 0.0), axis=0, keepdims=True
    ).astype(I32)
    p_exp_t[...] = one_hot(
        lax.div(source, CAP_G) * (BLK * CAP_G) + exp_k * CAP_G + lax.rem(source, CAP_G)
    )
    turn_id = lax.broadcasted_iota(I32, (16, ROWS), 0)
    at_group = (order == grp_n.astype(F32)) & (turn_id < NZ)
    position = jnp.sum(
        jnp.where(at_group, turn_id.astype(F32), 0.0), axis=0, keepdims=True
    ).astype(I32)
    p_grp_t[...] = one_hot(grp_k * TOK + grp_c * NZ + position)

    def dispatch(k, matrix):
        if k > 1:
            drain(zrecv.at[k], zr_sem.at[k])
        ysend[k] = reorder(matrix[...], zrecv[k].reshape(ROWS, LANES)).reshape(NY, BLK * CAP_E, LANES)
        start_y(ysend.at[k], yrecv.at[k], ys_sem.at[k], yr_sem.at[k])

    def forward(k):
        drain(yrecv.at[k], yr_sem.at[k])
        xsend[k] = reorder(p_mat[...], yrecv[k].reshape(ROWS, LANES)).reshape(2, FB * TOK, LANES)
        start_x(lambda x: xsend.at[k, lax.rem(x, 2)], xrecv.at[k], xs_sem.at[k], xr_sem.at[k])

    def collect(k):
        drain(xrecv.at[k], xr_sem.at[k])
        for x in range(NX):
            for b in range(FB):
                lhs[k, x * TOK : (x + 1) * TOK, b * LANES : (b + 1) * LANES] = xrecv[
                    k, x, b * TOK : (b + 1) * TOK, :
                ]

    def product(k, m):
        return jnp.dot(lhs[k], wbuf[m, k % 2], preferred_element_type=F32)

    def hand_over(k, m):
        for j in range(2):
            half = slice(j * QUART, (j + 1) * QUART)
            value = part[m, :, half] + jnp.dot(lhs[k], wbuf[m, k % 2, :, half], preferred_element_type=F32)
            part_out[m, j] = value.astype(BF16)
            send(
                part_out.at[m, j], part_in.at[m, my_h], ps_sem.at[m], pr_sem.at[m],
                place(my_y, 2 * j + 1 - my_k),
            )
            part[m, :, half] = value

    def whole(m):
        drain(part_in.at[m], pr_sem.at[m])
        return part[m] + jnp.concatenate([part_in[m, 0], part_in[m, 1]], axis=1).astype(F32)

    drain(zrecv.at[pl.ds(0, 2)], zr_sem.at[0])
    dispatch(0, p_exp)
    dispatch(1, p_exp)
    forward(0)
    dispatch(2, p_expw)
    forward(1)
    dispatch(3, p_expw)
    for m in range(3):
        kept[m].wait()
        drain(wbuf.at[m, core, :, pl.ds(other, QUART)], wb_sem.at[m])
        twins[m].start()
    forward(2)
    for m in range(3):
        twins[m].wait_recv()
    collect(0)
    for m in range(2):
        part[m] = product(0, m)
    collect(1)
    hand_over(1, 0)
    forward(3)
    hand_over(1, 1)
    collect(2)
    part[2] = product(2, 2)
    collect(3)
    hand_over(3, 2)

    pre_gate = whole(0)
    pre_up = whole(1)
    sig = jax.nn.sigmoid(pre_gate)
    gate_factor = pre_up * sig * (1.0 + pre_gate * (1.0 - sig))
    up_factor = pre_gate * sig
    grad_hid = whole(2)
    d_gate = (grad_hid * gate_factor).astype(BF16)
    d_up = (grad_hid * up_factor).astype(BF16)
    dims = (((1,), (1,)), ((), ()))
    for s in range(2):
        contrib = lax.dot_general(d_gate, wbuf[0, s], dims, preferred_element_type=F32)
        contrib = contrib + lax.dot_general(d_up, wbuf[1, s], dims, preferred_element_type=F32)
        contrib = contrib.astype(BF16)
        for x in range(NX):
            for b in range(FB):
                rsend[s, x, b * TOK : (b + 1) * TOK, :] = contrib[
                    x * TOK : (x + 1) * TOK, b * LANES : (b + 1) * LANES
                ]
        start_x(lambda x: rsend.at[s, x], rrecv.at[s], rs_sem.at[s], rr_sem.at[s])

    for s in range(2):
        drain(rrecv.at[s], rr_sem.at[s])
        summed = [(rrecv[s, f].astype(F32) + rrecv[s, f + 2].astype(F32)).astype(BF16) for f in range(2)]
        qsend[s] = reorder(p_mat_t[...], jnp.concatenate(summed, axis=0)).reshape(NY, BLK * CAP_E, LANES)
        start_y(qsend.at[s], qrecv.at[s], qs_sem.at[s], qr_sem.at[s])
    for s in range(2):
        drain(qrecv.at[s], qr_sem.at[s])
        bsend[s] = reorder(p_exp_t[...], qrecv[s].reshape(ROWS, LANES)).reshape(NZ, BLK * CAP_G, LANES)
        start_z(bsend.at[s], brecv.at[s], bs_sem.at[s], br_sem.at[s])
    drain(zsend.at[pl.ds(0, 2), pl.ds(0, NZ - 1)], zs_sem.at[0])
    for k in range(4):
        if k > 1:
            drain(zsend.at[k, pl.ds(0, NZ - 1)], zs_sem.at[k])
        drain(ysend.at[k, pl.ds(0, NY - 1)], ys_sem.at[k])
        drain(xrecv.at[k, pl.ds(0, NX - 1)], xs_sem.at[k])
    for s in range(2):
        drain(rsend.at[s, pl.ds(0, NX - 1)], rs_sem.at[s])
        drain(qsend.at[s, pl.ds(0, NY - 1)], qs_sem.at[s])
    for m in range(3):
        drain(part_out.at[m], ps_sem.at[m])
        twins[m].wait_send()

        @pl.when(my_k == 1)
        def _():
            swapped[m].wait_send()
    for s in range(2):
        drain(brecv.at[s], br_sem.at[s])
        result = reorder(p_grp_t[...], brecv[s].reshape(ROWS, LANES))
        for k, (f, b) in enumerate(blocks()):
            out_ref[:, feature(f, s, b)] = result[k * TOK : (k + 1) * TOK, :]
    for s in range(2):
        drain(bsend.at[s, pl.ds(0, NZ - 1)], bs_sem.at[s])


def per_device(inputs_x, grad_out, group_order, route_picks, gate_weights, w_gate, w_up, w_down):
    hbm = pl.BlockSpec(memory_space=pltpu.HBM)
    square = pltpu.VMEM((ROWS, ROWS), BF16)
    dma = pltpu.SemaphoreType.DMA
    z_buf, y_buf, x_buf = (NZ, BLK * CAP_G, LANES), (NY, BLK * CAP_E, LANES), (NX, FB * TOK, LANES)
    return pl.pallas_call(
        kernel,
        out_shape=jax.ShapeDtypeStruct(inputs_x.shape, BF16),
        in_specs=[hbm] * 8,
        out_specs=pl.BlockSpec(memory_space=pltpu.VMEM),
        scratch_shapes=[
            pltpu.VMEM((1, NZ), I32),
            pltpu.VMEM((1, TOK), I32),
            pltpu.VMEM((1, TOK), BF16),
            pltpu.VMEM((2, TOK, 4 * HALF), BF16),
            pltpu.VMEM((2, ROWS, 2 * LANES), BF16),
            pltpu.VMEM((4, *z_buf), BF16),
            pltpu.VMEM((4, *z_buf), BF16),
            pltpu.VMEM((4, *y_buf), BF16),
            pltpu.VMEM((4, *y_buf), BF16),
            pltpu.VMEM((4, 2, FB * TOK, LANES), BF16),
            pltpu.VMEM((4, *x_buf), BF16),
            pltpu.VMEM((4, NX * TOK, HALF), BF16),
            pltpu.VMEM((3, 2, HALF, HALF), BF16),
            pltpu.VMEM((3, NX * TOK, HALF), F32),
            pltpu.VMEM((3, 2, NX * TOK, QUART), BF16),
            pltpu.VMEM((3, 2, NX * TOK, QUART), BF16),
            pltpu.VMEM((2, *x_buf), BF16),
            pltpu.VMEM((2, *x_buf), BF16),
            pltpu.VMEM((2, *y_buf), BF16),
            pltpu.VMEM((2, *y_buf), BF16),
            pltpu.VMEM((2, *z_buf), BF16),
            pltpu.VMEM((2, *z_buf), BF16),
            square, square, square, square, square, square, square,
            dma((5,)), dma((3,)), dma((3,)), dma((3,)), dma((3,)), dma((3,)),
            dma((4,)), dma((4,)), dma((4,)), dma((4,)), dma((4,)), dma((4,)),
            dma((3,)), dma((3,)), dma((2,)), dma((2,)), dma((2,)), dma((2,)), dma((2,)), dma((2,)),
        ],
        compiler_params=pltpu.CompilerParams(
            collective_id=0, has_side_effects=True, vmem_limit_bytes=54886 * 2**10
        ),
    )(
        group_order, route_picks.reshape(1, TOK), gate_weights.reshape(1, TOK), inputs_x, grad_out,
        w_gate, w_up, w_down,
    )


def solution(mesh):
    placed = P(("node", "local"), None)
    return jax.shard_map(
        per_device, mesh=mesh, in_specs=(placed,) * 8, out_specs=placed, check_vma=False
    )
```
